512 devices in a mesh: dp: 16 (over x, y_hi, core), space: 32 (over y_lo, z).
Axes of the slice: x: 4, y: 4 (y_hi: 2, y_lo: 2; y = y_hi * 2 + y_lo), z: 16, core: 2. Of those that a mesh axis runs over, the one named last changes fastest.
Arguments:
- queries: bfloat16 [16, 1120, 8192], P('dp', None, 'space'), may hold values from -6 to 6
- keys: bfloat16 [16, 1120, 8192], P('dp', None, 'space'), may hold values from -6 to 6
- values: bfloat16 [16, 1120, 8192], P('dp', None, 'space'), may hold values from -5.5 to 5.5
- out_grad: bfloat16 [16, 1120, 8192], P('dp', None, 'space'), may hold values from -6 to 6
- q_gain: float32 [1120], replicated, may hold values from 0.5 to 1.5
- k_gain: float32 [1120], replicated, may hold values from 0.5 to 1.5
Outputs:
- grad_queries: bfloat16 [16, 1120, 8192], P('dp', None, 'space')
- grad_keys: bfloat16 [16, 1120, 8192], P('dp', None, 'space')
- grad_values: bfloat16 [16, 1120, 8192], P('dp', None, 'space')
- grad_q_gain: float32 [1120], replicated
- grad_k_gain: float32 [1120], replicated
The draws below stay inside these ranges and needn't reach their ends.
All inputs are finite; a program needn't handle non-finite values.
Results may differ from the reference program's by a relative error of at most 0.0055.
Values sent between devices are 32-bit elements; how exact they have to be, the bound alone decides.
A program may use at most 64 MiB of HBM per device.

```python
import math
import jax
import jax.numpy as jnp
from jax import lax

HEADS = 10
HEAD_DIM = 112
CH = 1120
TOKENS = 8192
SAMPLES = 16


def draw_values(key, part):
    key = jax.random.fold_in(key, 7)
    key_mean, key_noise = jax.random.split(key, 2)
    means = jax.random.uniform(key_mean, (SAMPLES, CH, 1), jnp.float32, -1.5, 1.5)
    drawn = means + jax.random.truncated_normal(key_noise, -4.0, 4.0, (SAMPLES, CH, TOKENS), jnp.float32)
    return drawn.astype(jnp.bfloat16)


def level_of(key, shape, shards, least, largest):
    def one(position, shards_of):
        heights = jax.random.uniform(jax.random.fold_in(jax.random.fold_in(key, 6), position), (shards_of,), jnp.float32, least / len(shards), largest / len(shards))
        return jnp.repeat(jnp.exp(heights), shape[position] // shards_of).reshape((-1,) + (1,) * (len(shape) - position - 1))

    level = one(*shards[0])
    for cut in shards[1:]:
        level = level * one(*cut)
    return level


def normal_values(stream_key, shape, scale, limit, cuts=(), dtype=jnp.bfloat16):
    entries = scale * jax.random.normal(stream_key, shape, jnp.float32)
    if cuts:
        entries = entries * level_of(stream_key, shape, cuts, -0.22, 0.18)
    return jnp.clip(entries, -limit, limit).astype(dtype)


def setup_inputs(seed: int = 0) -> dict:
    splits = jax.random.split(jax.random.key(seed), 7)
    queries = normal_values(splits[0], (SAMPLES, CH, TOKENS), 1.0, 6.0, ((0, 16), (2, 32)))
    keys = normal_values(splits[1], (SAMPLES, CH, TOKENS), 1.0, 6.0, ((0, 16), (2, 32)))
    values = draw_values(jax.random.fold_in(splits[6], 71), 0)
    out_grad = normal_values(splits[3], (SAMPLES, CH, TOKENS), 1.0, 6.0, ((0, 16), (2, 32)))
    q_gain = jnp.clip(1.0 + 0.1 * jax.random.normal(splits[4], (CH,), jnp.float32), 0.5, 1.5)
    k_gain = jnp.clip(1.0 + 0.1 * jax.random.normal(splits[5], (CH,), jnp.float32), 0.5, 1.5)
    return {"queries": queries, "keys": keys, "values": values, "out_grad": out_grad, "q_gain": q_gain, "k_gain": k_gain}


norm_eps = 1e-06
denom_eps = 1e-06
highest = lax.Precision.HIGHEST

def normalize(inputs, gain):
    floats = inputs.astype(jnp.float32).reshape(HEADS, HEAD_DIM, -1)
    inverse = lax.rsqrt(lax.optimization_barrier(jnp.mean(floats * floats, axis=1, keepdims=True)) + norm_eps)
    unit = floats * inverse
    return (unit, inverse, unit * gain.reshape(HEADS, HEAD_DIM, 1))

def features(normed):
    rounded = jnp.maximum(normed, 0.0).astype(jnp.bfloat16)
    rounded = lax.optimization_barrier(rounded)
    return rounded.astype(jnp.float32)

def norm_backward(grad_normed, unit, inverse, gain):
    upstream = grad_normed * gain.reshape(HEADS, HEAD_DIM, 1)
    grad_in = inverse * (upstream - unit * lax.optimization_barrier(jnp.mean(upstream * unit, axis=1, keepdims=True)))
    return (grad_in.reshape(HEADS * HEAD_DIM, -1).astype(jnp.bfloat16), lax.optimization_barrier(jnp.sum(grad_normed * unit, axis=2)))

def reference(queries, keys, values, out_grad, q_gain, k_gain):
    loss_scale = math.sqrt(TOKENS)

    def one_clip(pieces):
        query_in, key_in, value_in, grad_in = pieces
        unit_query, inverse_query, normed_query = normalize(query_in, q_gain)
        unit_key, inverse_key, normed_key = normalize(key_in, k_gain)
        feature_query = features(normed_query)
        feature_key = features(normed_key)
        value_heads = value_in.astype(jnp.float32).reshape(HEADS, HEAD_DIM, -1)
        grad_heads = grad_in.astype(jnp.float32).reshape(HEADS, HEAD_DIM, -1)
        state = jnp.einsum('hct,hdt->hcd', feature_key, value_heads, precision=highest)
        key_total = lax.optimization_barrier(jnp.sum(feature_key, axis=2))
        denominator = jnp.einsum('hct,hc->ht', feature_query, key_total, precision=highest) + denom_eps
        attended = jnp.einsum('hct,hcd->hdt', feature_query, state, precision=highest) / denominator[:, None, :]
        scaled = loss_scale * grad_heads / denominator[:, None, :]
        projected = lax.optimization_barrier(jnp.sum(attended * scaled, axis=1))
        grad_state = jnp.einsum('hct,hdt->hcd', feature_query, scaled, precision=highest)
        grad_key_total = -jnp.einsum('hct,ht->hc', feature_query, projected, precision=highest)
        grad_feat_q = jnp.einsum('hcd,hdt->hct', state, scaled, precision=highest) - key_total[:, :, None] * projected[:, None, :]
        grad_feat_k = jnp.einsum('hcd,hdt->hct', grad_state, value_heads, precision=highest) + grad_key_total[:, :, None]
        grad_value = jnp.einsum('hcd,hct->hdt', grad_state, feature_key, precision=highest)
        grad_value = grad_value.reshape(HEADS * HEAD_DIM, -1).astype(jnp.bfloat16)
        grad_normed_q = jnp.where(normed_query > 0, grad_feat_q, 0.0)
        grad_normed_k = jnp.where(normed_key > 0, grad_feat_k, 0.0)
        grad_query, part_query = norm_backward(grad_normed_q, unit_query, inverse_query, q_gain)
        grad_key, part_key = norm_backward(grad_normed_k, unit_key, inverse_key, k_gain)
        return (grad_query, grad_key, grad_value, part_query, part_key)
    grad_queries, grad_keys, grad_values, parts_q, parts_k = lax.map(one_clip, (queries, keys, values, out_grad))
    divisor = math.sqrt(SAMPLES * TOKENS)
    grad_q_gain = (lax.optimization_barrier(jnp.sum(parts_q, axis=0)) / divisor).reshape(HEADS * HEAD_DIM)
    grad_k_gain = (lax.optimization_barrier(jnp.sum(parts_k, axis=0)) / divisor).reshape(HEADS * HEAD_DIM)
    return (grad_queries, grad_keys, grad_values, grad_q_gain, grad_k_gain)
```

```python
import math

import jax
import jax.numpy as jnp
from jax import lax
from jax.experimental import pallas as pl
from jax.experimental.pallas import tpu as pltpu
from jax.sharding import PartitionSpec as P

HEADS = 10
HEAD_DIM = 112
CH = HEADS * HEAD_DIM
LANES = 128
SPLIT_HEAD = 7
SPARE = LANES - HEAD_DIM
HOSTS = HEAD_DIM // SPARE
ROWS = 1024
PIECES = 4
PIECE = ROWS // PIECES
HALF = PIECE // 2
QUARTER = HALF // 4
OWN = QUARTER // 4
Y, Z = 2, 16

norm_eps = 1e-06
denom_eps = 1e-06
F32 = jnp.float32
BF16 = jnp.bfloat16
MESH = pl.DeviceIdType.MESH
NT = (((1,), (1,)), ((), ()))
NN = (((1,), (0,)), ((), ()))
TN = (((0,), (0,)), ((), ()))


def dot(a, b, dims):
    return lax.dot_general(a, b, dims, preferred_element_type=F32)


def split(x):
    high = x.astype(BF16)
    return high, (x - high.astype(F32)).astype(BF16)


def rows_of(head):
    return pl.ds(head * HEAD_DIM, HEAD_DIM)


def block_of(head):
    return pl.ds((head if head < SPLIT_HEAD else head - 1) * HEAD_DIM, HEAD_DIM)


def kernel(
    clip_tokens,
    all_rows,
    dps,
    q_hbm,
    k_hbm,
    v_hbm,
    g_hbm,
    gains_ref,
    gq_hbm,
    gk_hbm,
    gv_hbm,
    gain_out,
    q_in,
    k_in,
    v_in,
    g_in,
    feat_q,
    feat_k,
    inv_q,
    inv_k,
    rden,
    scaled_hi,
    scaled_lo,
    grad_f,
    out_q,
    out_k,
    out_v,
    gain_col,
    kt_col,
    part,
    recv_y,
    half,
    recv_w,
    quarter,
    recv_s,
    full,
    one_a,
    one_b,
    two_a,
    two_b,
    three,
    load_sem,
    store_sem,
    big_send,
    big_recv,
    small_send,
    small_recv,
):
    tokens = q_in.shape[1]
    dp = lax.axis_index("dp")
    space = lax.axis_index("space")
    y, z = space // Z, space % Z
    k4, g4 = z % 4, z // 4
    sign = 1 - 2 * (dp % 2)

    def at(dy, dz):
        return (dp, lax.rem(y + dy, Y) * Z + lax.rem(z + dz + 2 * Z, Z))

    loads = [
        pltpu.make_async_copy(src.at[0], dst, load_sem.at[i])
        for i, (src, dst) in enumerate(
            ((k_hbm, k_in), (v_hbm, v_in), (q_hbm, q_in), (g_hbm, g_in))
        )
    ]
    for load in loads:
        load.start()

    barrier = pltpu.get_barrier_semaphore()

    def cluster_peer(r):
        return (dp, lax.rem(y + r // 4, Y) * Z + g4 * 4 + lax.rem(k4 + r % 4, 4))

    greeted = 0
    for r in range(1, 8):
        pl.semaphore_signal(barrier, inc=1, device_id=cluster_peer(r), device_id_type=MESH)
        greeted += 1
    for dz in (1, -1, 2, -2, 4, -4, 8):
        pl.semaphore_signal(barrier, inc=1, device_id=at(0, dz), device_id_type=MESH)
        greeted += 1
    for r in range(1, dps):
        pl.semaphore_signal(
            barrier, inc=1, device_id=(lax.rem(dp + r, dps), space), device_id_type=MESH
        )
        greeted += 1

    lane = lax.broadcasted_iota(jnp.int32, (HEAD_DIM, LANES), 1)
    ones = jnp.ones((16, tokens), BF16)
    no_rows = jnp.zeros((SPARE, tokens), BF16)

    gain_col[...] = jnp.transpose(gains_ref[...])

    def q_gain(h):
        return gain_col[0:HEAD_DIM, h : h + 1]

    def k_gain(h):
        return gain_col[0:HEAD_DIM, 16 + h : 17 + h]

    def pad(x):
        return jnp.concatenate([x, no_rows], axis=0)

    def features(x_in, inv_ref, gain, feat_ref, h):
        x = x_in[rows_of(h), :].astype(F32)
        inverse = lax.rsqrt(jnp.sum(x * x, axis=0, keepdims=True) * (1.0 / HEAD_DIM) + norm_eps)
        inv_ref[h : h + 1, :] = inverse
        feat = jnp.maximum((x * inverse) * gain(h), 0.0).astype(BF16)
        feat_ref[rows_of(h), :] = feat
        return feat

    def place(a, h, block, spread):
        if h < HOSTS:
            moved = pltpu.roll(spread, (HEAD_DIM - SPARE * h) % LANES, 1)
            block = jnp.where(lane >= HEAD_DIM, moved, block)
        part[a, block_of(h), :] = block

    def take(a, h):
        if h != SPLIT_HEAD:
            return full[a, block_of(h), :][:, 0:HEAD_DIM]
        whole = jnp.zeros((HEAD_DIM, LANES), F32)
        for j in range(HOSTS):
            moved = pltpu.roll(full[a, block_of(j), :], (SPARE * j - HEAD_DIM) % LANES, 1)
            whole = jnp.where((lane >= SPARE * j) & (lane < SPARE * (j + 1)), moved, whole)
        return whole[:, 0:HEAD_DIM]

    order = [SPLIT_HEAD] + [h for h in range(HEADS) if h != SPLIT_HEAD]
    tail = pl.ds((HEADS - 1) * HEAD_DIM, ROWS - (HEADS - 1) * HEAD_DIM)

    def big(a, p, slot, src, dst, peer):
        return pltpu.make_async_remote_copy(
            src_ref=src,
            dst_ref=dst,
            send_sem=big_send.at[a, p, slot],
            recv_sem=big_recv.at[a, p, slot],
            device_id=peer,
            device_id_type=MESH,
        )

    sent = []

    def go(copies):
        for copy in copies:
            copy.start()
            sent.append(copy)
        return copies

    def land(copies):
        for copy in copies:
            copy.wait_recv()

    window = (sign, -sign, -2 * sign)
    stride = (4, 12, 8)

    def rs_y(a, p):
        other = lax.rem(y + 1, Y)
        src = part.at[a, pl.ds(pl.multiple_of(p * PIECE + other * HALF, HALF), HALF)]
        return go([big(a, p, 0, src, recv_y.at[a, p], at(1, 0))])

    def rs_w(a, p, came):
        land(came)
        mine = pl.ds(pl.multiple_of(p * PIECE + y * HALF, HALF), HALF)
        half[a, p] = part[a, mine, :] + recv_y[a, p]
        copies = []
        for m, dz in enumerate(window):
            kind = lax.rem(z + dz + Z, 4)
            src = half.at[a, p, pl.ds(pl.multiple_of(kind * QUARTER, QUARTER), QUARTER)]
            copies.append(big(a, p, 1 + m, src, recv_w.at[a, p, m], at(0, dz)))
        return go(copies)

    def rs_s(a, p, came):
        land(came)
        mine = pl.ds(pl.multiple_of(k4 * QUARTER, QUARTER), QUARTER)
        quarter[a, p] = (half[a, p, mine, :] + recv_w[a, p, 0]) + (
            recv_w[a, p, 1] + recv_w[a, p, 2]
        )
        copies = []
        for m, dz in enumerate(stride):
            group = lax.rem(g4 + dz // 4, 4)
            src = quarter.at[a, p, pl.ds(pl.multiple_of(group * OWN, OWN), OWN)]
            copies.append(big(a, p, 4 + m, src, recv_s.at[a, p, m], at(0, dz)))
        return go(copies)

    def ag_s(a, p, came):
        land(came)
        own = pl.ds(pl.multiple_of(g4 * OWN, OWN), OWN)
        place_own = pl.ds(
            pl.multiple_of(p * PIECE + y * HALF + k4 * QUARTER + g4 * OWN, OWN), OWN
        )
        full[a, place_own, :] = (quarter[a, p, own, :] + recv_s[a, p, 0]) + (
            recv_s[a, p, 1] + recv_s[a, p, 2]
        )
        ref = full.at[a, place_own]
        return go([big(a, p, 7 + m, ref, ref, at(0, dz)) for m, dz in enumerate(stride)])

    def ag_w(a, p, came):
        land(came)
        ref = full.at[
            a, pl.ds(pl.multiple_of(p * PIECE + y * HALF + k4 * QUARTER, QUARTER), QUARTER)
        ]
        return go([big(a, p, 10 + m, ref, ref, at(0, dz)) for m, dz in enumerate(window)])

    def ag_y(a, p, came):
        land(came)
        ref = full.at[a, pl.ds(pl.multiple_of(p * PIECE + y * HALF, HALF), HALF)]
        return go([big(a, p, 13, ref, ref, at(1, 0))])

    def small(slot, ref, peer):
        return pltpu.make_async_remote_copy(
            src_ref=ref,
            dst_ref=ref,
            send_sem=small_send.at[slot],
            recv_sem=small_recv.at[slot],
            device_id=peer,
            device_id_type=MESH,
        )

    def small_cluster(base, buf):
        ref = buf.at[y * 4 + k4]
        return go([small(base + r, ref, cluster_peer(r)) for r in range(1, 8)])

    def small_stride(base, came, buf_a, buf_b):
        land(came)
        total = buf_a[0]
        for e in range(1, 8):
            total = total + buf_a[e]
        buf_b[g4] = total
        ref = buf_b.at[g4]
        return go([small(base + m, ref, at(0, dz)) for m, dz in enumerate(stride)])

    def small_done(came, buf_b):
        land(came)
        return (buf_b[0] + buf_b[1]) + (buf_b[2] + buf_b[3])

    cell = y * 4 + k4
    one_a[cell] = jnp.zeros_like(one_a[cell])
    two_a[cell] = jnp.zeros_like(two_a[cell])
    part[0, tail, :] = jnp.zeros((tail.size, LANES), F32)
    part[1, tail, :] = jnp.zeros((tail.size, LANES), F32)

    loads[0].wait()
    loads[1].wait()
    spread = None
    for h in order:
        feat = features(k_in, inv_k, k_gain, feat_k, h)
        one_a[cell, h : h + 1, 0:HEAD_DIM] = dot(ones, feat, NT)[0:1]
        block = dot(feat, pad(v_in[rows_of(h), :]), NT)
        if h == SPLIT_HEAD:
            spread = block
        else:
            place(0, h, block, spread)
    loads[2].wait()
    for h in order:
        features(q_in, inv_q, q_gain, feat_q, h)
    loads[3].wait()

    pl.semaphore_wait(barrier, greeted)
    pieces = range(PIECES)
    ar1 = small_cluster(0, one_a)
    s = [rs_y(0, p) for p in pieces]
    ar1 = small_stride(8, ar1, one_a, one_b)
    s = [rs_w(0, p, s[p]) for p in pieces]
    s = [rs_s(0, p, s[p]) for p in pieces]

    key_total = small_done(ar1, one_b)
    kt_col[...] = jnp.transpose(key_total)
    kt_hi, kt_rest = split(key_total)
    kt_mid = kt_rest
    kt_lo = (key_total - kt_hi.astype(F32) - kt_mid.astype(F32)).astype(BF16)
    kt3 = jnp.concatenate([kt_hi, kt_mid, kt_lo], axis=0)[:, 0:HEAD_DIM]
    loss_scale = math.sqrt(clip_tokens)
    for h in order:
        feat = feat_q[rows_of(h), :]
        terms = dot(kt3, feat, NN)
        denominator = (
            terms[h : h + 1] + (terms[16 + h : 17 + h] + terms[32 + h : 33 + h])
        ) + denom_eps
        inverse = 1.0 / denominator
        rden[h : h + 1, :] = inverse
        scaled = g_in[rows_of(h), :].astype(F32) * (loss_scale * inverse)
        high, low = split(scaled)
        scaled_hi[rows_of(h), :] = high
        scaled_lo[rows_of(h), :] = low
        block = dot(feat, pad(high), NT) + dot(feat, pad(low), NT)
        if h == SPLIT_HEAD:
            spread = block
        else:
            place(1, h, block, spread)

    g = [rs_y(1, p) for p in pieces]
    s = [ag_s(0, p, s[p]) for p in pieces]
    g = [rs_w(1, p, g[p]) for p in pieces]
    s = [ag_w(0, p, s[p]) for p in pieces]
    g = [rs_s(1, p, g[p]) for p in pieces]
    s = [ag_y(0, p, s[p]) for p in pieces]
    for p in pieces:
        land(s[p])

    for h in range(HEADS):
        feat = feat_q[rows_of(h), :]
        high, low = scaled_hi[rows_of(h), :], scaled_lo[rows_of(h), :]
        state_hi, state_lo = split(take(0, h))
        grad = dot(state_hi, high, NN) + (dot(state_lo, high, NN) + dot(state_hi, low, NN))
        feat_f = feat.astype(F32)
        projected = jnp.sum(feat_f * grad, axis=0, keepdims=True) * rden[h : h + 1, :]
        grad = grad - kt_col[0:HEAD_DIM, h : h + 1] * projected
        grad_f[rows_of(h), :] = grad
        p_hi, p_lo = split(-projected)
        two_a[cell, h : h + 1, 0:HEAD_DIM] = (
            dot(jnp.broadcast_to(p_hi, (16, tokens)), feat, NT)
            + dot(jnp.broadcast_to(p_lo, (16, tokens)), feat, NT)
        )[0:1]
        e_hi, e_lo = split(feat_f * grad)
        two_a[cell, HEADS + h : HEADS + h + 1, 0:HEAD_DIM] = (
            dot(ones, e_hi, NT) + dot(ones, e_lo, NT)
        )[0:1]
    ar2 = small_cluster(16, two_a)

    g = [ag_s(1, p, g[p]) for p in pieces]

    def norm_backward(x_in, inv_ref, gain, feat, grad, out, h):
        inverse = inv_ref[h : h + 1, :]
        unit = x_in[rows_of(h), :].astype(F32) * inverse
        upstream = jnp.where(feat > 0, grad, 0.0) * gain(h)
        mean = jnp.sum(upstream * unit, axis=0, keepdims=True) * (1.0 / HEAD_DIM)
        out[rows_of(h), :] = (inverse * (upstream - unit * mean)).astype(BF16)

    def grad_queries(heads):
        for h in heads:
            feat = feat_q[rows_of(h), :].astype(F32)
            norm_backward(q_in, inv_q, q_gain, feat, grad_f[rows_of(h), :], out_q, h)

    grad_queries(range(HEADS))
    store_q = pltpu.make_async_copy(out_q, gq_hbm.at[0], store_sem.at[0])
    store_q.start()
    ar2 = small_stride(24, ar2, two_a, two_b)
    g = [ag_w(1, p, g[p]) for p in pieces]
    g = [ag_y(1, p, g[p]) for p in pieces]
    for p in pieces:
        land(g[p])

    for h in range(HEADS):
        gs_hi, gs_lo = split(take(1, h))
        value = v_in[rows_of(h), :]
        feat = feat_k[rows_of(h), :]
        out_v[rows_of(h), :] = (dot(gs_hi, feat, TN) + dot(gs_lo, feat, TN)).astype(BF16)
        grad_f[rows_of(h), :] = dot(gs_hi, value, NN) + dot(gs_lo, value, NN)
    store_v = pltpu.make_async_copy(out_v, gv_hbm.at[0], store_sem.at[1])
    store_v.start()

    total = small_done(ar2, two_b)
    three[dp] = total
    ref = three.at[dp]
    ar3 = go([small(32 + r, ref, (lax.rem(dp + r, dps), space)) for r in range(1, dps)])
    gkt_col = jnp.transpose(total)
    for h in range(HEADS):
        feat = feat_k[rows_of(h), :].astype(F32)
        grad = grad_f[rows_of(h), :] + gkt_col[0:HEAD_DIM, h : h + 1]
        norm_backward(k_in, inv_k, k_gain, feat, grad, out_k, h)
    store_k = pltpu.make_async_copy(out_k, gk_hbm.at[0], store_sem.at[2])
    store_k.start()

    land(ar3)
    total = three[0]
    for r in range(1, dps):
        total = total + three[r]
    gain_sum = total[HEADS : 2 * HEADS, 0:HEAD_DIM] * (1.0 / math.sqrt(all_rows))
    gain_out[0] = gain_sum / gains_ref[0:HEADS, 0:HEAD_DIM]
    gain_out[1] = gain_sum / gains_ref[16 : 16 + HEADS, 0:HEAD_DIM]

    for copy in sent:
        copy.wait_send()
    store_q.wait()
    store_v.wait()
    store_k.wait()


def local(queries, keys, values, out_grad, q_gain, k_gain):
    tokens = queries.shape[2]
    dps = lax.axis_size("dp")
    clip_tokens = tokens * lax.axis_size("space")
    all_rows = clip_tokens * dps * queries.shape[0]
    gains = jnp.concatenate(
        [
            jnp.pad(g.reshape(HEADS, HEAD_DIM), ((0, 16 - HEADS), (0, SPARE)), constant_values=1.0)
            for g in (q_gain, k_gain)
        ]
    )
    anywhere = pl.BlockSpec(memory_space=pl.ANY)
    here = pl.BlockSpec(memory_space=pltpu.VMEM)
    big = jax.ShapeDtypeStruct(queries.shape, BF16)
    vm = pltpu.VMEM
    dma = pltpu.SemaphoreType.DMA

    def run(*refs):
        kernel(clip_tokens, all_rows, dps, *refs)

    grad_q, grad_k, grad_v, gain_grads = pl.pallas_call(
        run,
        out_shape=(big, big, big, jax.ShapeDtypeStruct((2, HEADS, HEAD_DIM), F32)),
        in_specs=[anywhere] * 4 + [here],
        out_specs=(anywhere, anywhere, anywhere, here),
        scratch_shapes=[
            vm((CH, tokens), BF16),
            vm((CH, tokens), BF16),
            vm((CH, tokens), BF16),
            vm((CH, tokens), BF16),
            vm((CH, tokens), BF16),
            vm((CH, tokens), BF16),
            vm((16, tokens), F32),
            vm((16, tokens), F32),
            vm((16, tokens), F32),
            vm((CH, tokens), BF16),
            vm((CH, tokens), BF16),
            vm((CH, tokens), F32),
            vm((CH, tokens), BF16),
            vm((CH, tokens), BF16),
            vm((CH, tokens), BF16),
            vm((LANES, 32), F32),
            vm((LANES, 16), F32),
            vm((2, ROWS, LANES), F32),
            vm((2, PIECES, HALF, LANES), F32),
            vm((2, PIECES, HALF, LANES), F32),
            vm((2, PIECES, 3, QUARTER, LANES), F32),
            vm((2, PIECES, QUARTER, LANES), F32),
            vm((2, PIECES, 3, OWN, LANES), F32),
            vm((2, ROWS, LANES), F32),
            vm((8, 16, LANES), F32),
            vm((4, 16, LANES), F32),
            vm((8, 24, LANES), F32),
            vm((4, 24, LANES), F32),
            vm((dps, 24, LANES), F32),
            dma((4,)),
            dma((3,)),
            dma((2, PIECES, 14)),
            dma((2, PIECES, 14)),
            dma((32 + 16,)),
            dma((32 + 16,)),
        ],
        compiler_params=pltpu.CompilerParams(
            collective_id=0, has_side_effects=True, vmem_limit_bytes=48 << 20
        ),
        name="linear_attention_backward",
    )(queries, keys, values, out_grad, gains)
    return (
        grad_q,
        grad_k,
        grad_v,
        gain_grads[0].reshape(CH),
        gain_grads[1].reshape(CH),
    )


def solution(mesh):
    whole = P("dp", None, "space")
    return jax.shard_map(
        local,
        mesh=mesh,
        in_specs=(whole, whole, whole, whole, P(), P()),
        out_specs=(whole, whole, whole, P(), P()),
        check_vma=False,
    )
```

```python
import math

import jax
import jax.numpy as jnp
from jax import lax
from jax.experimental import pallas as pl
from jax.experimental.pallas import tpu as pltpu
from jax.sharding import PartitionSpec as P

HEADS = 10
HEAD_DIM = 112
CH = HEADS * HEAD_DIM
LANES = 128
SPLIT_HEAD = 7
SPARE = LANES - HEAD_DIM
HOSTS = HEAD_DIM // SPARE
ROWS = 1024
PIECES = 4
PIECE = ROWS // PIECES
HALF = PIECE // 2
QUARTER = HALF // 4
OWN = QUARTER // 4
CLASS = PIECE // 4
KINDS = ("a", "a", "a", "b")
STAGES = 6
VMEM_BYTES = 62 << 20
CUTS = 2
Y, Z = 2, 16

norm_eps = 1e-06
denom_eps = 1e-06
F32 = jnp.float32
BF16 = jnp.bfloat16
MESH = pl.DeviceIdType.MESH
NT = (((1,), (1,)), ((), ()))
NN = (((1,), (0,)), ((), ()))
TN = (((0,), (0,)), ((), ()))


def dot(a, b, dims):
    return lax.dot_general(a, b, dims, preferred_element_type=F32)


def split(x):
    high = x.astype(BF16)
    return high, (x - high.astype(F32)).astype(BF16)


def rows_of(head):
    return pl.ds(head * HEAD_DIM, HEAD_DIM)


def block_of(head):
    return pl.ds((head if head < SPLIT_HEAD else head - 1) * HEAD_DIM, HEAD_DIM)


def kernel(
    clip_tokens,
    all_rows,
    dps,
    q_hbm,
    k_hbm,
    v_hbm,
    g_hbm,
    qg_hbm,
    kg_hbm,
    gq_hbm,
    gk_hbm,
    gv_hbm,
    gain_q_hbm,
    gain_k_hbm,
    q_in,
    k_in,
    v_in,
    g_in,
    qg_ref,
    kg_ref,
    gain_q_out,
    gain_k_out,
    feat_q,
    feat_k,
    inv_q,
    inv_k,
    rden,
    scaled_hi,
    scaled_lo,
    grad_f,
    out_q,
    out_k,
    out_v,
    gain_row,
    gain_col,
    kt_col,
    part,
    recv_y,
    half,
    recv_w,
    quarter,
    recv_s,
    full,
    one_a,
    one_b,
    two_a,
    two_b,
    three,
    sizes,
    load_sem,
    store_sem,
    send_sem,
    big_recv,
    small_recv,
    far_sem,
):
    tokens = q_in.shape[1]
    dp = lax.axis_index("dp")
    space = lax.axis_index("space")
    y, z = space // Z, space % Z
    k4, g4 = z % 4, z // 4
    sign = 1 - 2 * (dp % 2)

    def at(dy, dz):
        return (dp, lax.rem(y + dy, Y) * Z + lax.rem(z + dz + 2 * Z, Z))

    loads = [
        pltpu.make_async_copy(src, dst, load_sem.at[i])
        for i, (src, dst) in enumerate(
            (
                (k_hbm.at[0], k_in),
                (kg_hbm, kg_ref),
                (qg_hbm, qg_ref),
                (v_hbm.at[0], v_in),
                (q_hbm.at[0], q_in),
                (g_hbm.at[0], g_in),
            )
        )
    ]
    for load in loads:
        load.start()

    barrier = pltpu.get_barrier_semaphore()

    def cluster_peer(r):
        return (dp, lax.rem(y + r // 4, Y) * Z + g4 * 4 + lax.rem(k4 + r % 4, 4))

    greeted = 0
    for r in range(1, 8):
        pl.semaphore_signal(barrier, inc=1, device_id=cluster_peer(r), device_id_type=MESH)
        greeted += 1
    for dy, dz in ((0, 1), (0, -1), (0, 2), (0, -2), (0, 4), (0, -4), (1, 4), (1, -4)):
        pl.semaphore_signal(barrier, inc=1, device_id=at(dy, dz), device_id_type=MESH)
        greeted += 1
    for r in range(1, dps):
        pl.semaphore_signal(
            barrier, inc=1, device_id=(lax.rem(dp + r, dps), space), device_id_type=MESH
        )
        greeted += 1

    lane = lax.broadcasted_iota(jnp.int32, (HEAD_DIM, LANES), 1)
    ones = jnp.ones((16, tokens), BF16)
    no_rows = jnp.zeros((SPARE, tokens), BF16)

    def q_gain(h):
        return gain_col[0:HEAD_DIM, h : h + 1]

    def k_gain(h):
        return gain_col[0:HEAD_DIM, 16 + h : 17 + h]

    def pad(x):
        return jnp.concatenate([x, no_rows], axis=0)

    def features(x_in, inv_ref, gain, feat_ref, h):
        x = x_in[rows_of(h), :].astype(F32)
        inverse = lax.rsqrt(jnp.sum(x * x, axis=0, keepdims=True) * (1.0 / HEAD_DIM) + norm_eps)
        inv_ref[h : h + 1, :] = inverse
        feat = jnp.maximum((x * inverse) * gain(h), 0.0).astype(BF16)
        feat_ref[rows_of(h), :] = feat
        return feat

    def place(a, h, block, spread):
        if h < HOSTS:
            moved = pltpu.roll(spread, (HEAD_DIM - SPARE * h) % LANES, 1)
            block = jnp.where(lane >= HEAD_DIM, moved, block)
        part[a, block_of(h), :] = block

    def take(a, h):
        if h != SPLIT_HEAD:
            return full[a, block_of(h), :][:, 0:HEAD_DIM]
        whole = jnp.zeros((HEAD_DIM, LANES), F32)
        for j in range(HOSTS):
            moved = pltpu.roll(full[a, block_of(j), :], (SPARE * j - HEAD_DIM) % LANES, 1)
            whole = jnp.where((lane >= SPARE * j) & (lane < SPARE * (j + 1)), moved, whole)
        return whole[:, 0:HEAD_DIM]

    order = [SPLIT_HEAD] + [h for h in range(HEADS) if h != SPLIT_HEAD]
    tail = pl.ds((HEADS - 1) * HEAD_DIM, ROWS - (HEADS - 1) * HEAD_DIM)

    sent = [0]

    def go(recv_sem, copies):
        rows = 0
        for src, dst, peer in copies:
            pltpu.make_async_remote_copy(
                src_ref=src,
                dst_ref=dst,
                send_sem=send_sem,
                recv_sem=recv_sem,
                device_id=peer,
                device_id_type=MESH,
            ).start()
            rows += src.shape[0]
        sent[0] += rows
        return recv_sem, rows

    def wait_rows(sem, rows):
        ref = sizes.at[pl.ds(0, rows)]
        pltpu.make_async_copy(ref, ref, sem).wait()

    def land(came):
        wait_rows(*came)

    window = (sign, -sign, -2 * sign)
    stride = (4, 12, 8)
    both = [(r // 4, 4 * (r % 4)) for r in range(1, 8)]

    def near(start, size):
        return pl.ds(pl.multiple_of(start, size), size)

    def a_rs_y(a, p, came):
        src = part.at[a, near(p * PIECE + lax.rem(y + 1, Y) * HALF, HALF)]
        return go(big_recv.at[a, p, 0], [(src, recv_y.at[a, p], at(1, 0))])

    def a_rs_w(a, p, came):
        land(came)
        half[a, p] = part[a, near(p * PIECE + y * HALF, HALF), :] + recv_y[a, p]
        copies = []
        for m, dz in enumerate(window):
            src = half.at[a, p, near(lax.rem(z + dz + Z, 4) * QUARTER, QUARTER)]
            dst = recv_w.at[a, p, m, pl.ds(0, QUARTER)]
            copies.append((src, dst, at(0, dz)))
        return go(big_recv.at[a, p, 1], copies)

    def a_rs_s(a, p, came):
        land(came)
        cut = pl.ds(0, QUARTER)
        quarter[a, p, cut, :] = (
            half[a, p, near(k4 * QUARTER, QUARTER), :] + recv_w[a, p, 0, cut, :]
        ) + (recv_w[a, p, 1, cut, :] + recv_w[a, p, 2, cut, :])
        copies = []
        for m, dz in enumerate(stride):
            src = quarter.at[a, p, near(lax.rem(g4 + dz // 4, 4) * OWN, OWN)]
            copies.append((src, recv_s.at[a, p, m], at(0, dz)))
        return go(big_recv.at[a, p, 2], copies)

    def a_ag_s(a, p, came):
        land(came)
        own = near(p * PIECE + y * HALF + k4 * QUARTER + g4 * OWN, OWN)
        full[a, own, :] = (quarter[a, p, near(g4 * OWN, OWN), :] + recv_s[a, p, 0]) + (
            recv_s[a, p, 1] + recv_s[a, p, 2]
        )
        ref = full.at[a, own]
        return go(big_recv.at[a, p, 3], [(ref, ref, at(0, dz)) for dz in stride])

    def a_ag_w(a, p, came):
        land(came)
        ref = full.at[a, near(p * PIECE + y * HALF + k4 * QUARTER, QUARTER)]
        return go(big_recv.at[a, p, 4], [(ref, ref, at(0, dz)) for dz in window])

    def a_ag_y(a, p, came):
        land(came)
        ref = full.at[a, near(p * PIECE + y * HALF, HALF)]
        return go(big_recv.at[a, p, 5], [(ref, ref, at(1, 0))])

    def b_rs_w(a, p, came):
        copies = []
        for m, dz in enumerate(window):
            src = part.at[a, near(p * PIECE + lax.rem(z + dz + Z, 4) * CLASS, CLASS)]
            copies.append((src, recv_w.at[a, p, m], at(0, dz)))
        return go(big_recv.at[a, p, 0], copies)

    def b_rs_s(a, p, came):
        land(came)
        quarter[a, p] = (
            part[a, near(p * PIECE + k4 * CLASS, CLASS), :] + recv_w[a, p, 0]
        ) + (recv_w[a, p, 1] + recv_w[a, p, 2])
        copies = []
        for m, (dy, dz) in enumerate(both):
            start = lax.rem(y + dy, Y) * (4 * OWN) + lax.rem(g4 + dz // 4, 4) * OWN
            src = quarter.at[a, p, near(start, OWN)]
            copies.append((src, recv_s.at[a, p, m], at(dy, dz)))
        return go(big_recv.at[a, p, 1], copies)

    def b_ag_s(a, p, came):
        land(came)
        start = y * (4 * OWN) + g4 * OWN
        total = quarter[a, p, near(start, OWN), :]
        for m in range(len(both)):
            total = total + recv_s[a, p, m]
        own = near(p * PIECE + k4 * CLASS + start, OWN)
        full[a, own, :] = total
        ref = full.at[a, own]
        return go(big_recv.at[a, p, 2], [(ref, ref, at(dy, dz)) for dy, dz in both])

    def b_ag_w(a, p, came):
        land(came)
        ref = full.at[a, near(p * PIECE + k4 * CLASS, CLASS)]
        return go(big_recv.at[a, p, 3], [(ref, ref, at(0, dz)) for dz in window])

    stages = {
        "a": (a_rs_y, a_rs_w, a_rs_s, a_ag_s, a_ag_w, a_ag_y),
        "b": (b_rs_w, b_rs_s, b_ag_s, b_ag_w),
    }
    under_way = {}

    def step(a, *pieces):
        for p in pieces:
            at_stage, came = under_way.get((a, p), (0, None))
            todo = stages[KINDS[p]]
            if at_stage < len(todo):
                came = todo[at_stage](a, p, came)
            else:
                land(came)
            under_way[a, p] = (at_stage + 1, came)

    def small_cluster(slot, buf):
        ref = buf.at[y * 4 + k4]
        return go(small_recv.at[slot], [(ref, ref, cluster_peer(r)) for r in range(1, 8)])

    def small_stride(slot, came, buf_a, buf_b):
        land(came)
        total = buf_a[0]
        for e in range(1, 8):
            total = total + buf_a[e]
        buf_b[g4] = total
        ref = buf_b.at[g4]
        return go(small_recv.at[slot], [(ref, ref, at(0, dz)) for dz in stride])

    def small_done(came, buf_b):
        land(came)
        return (buf_b[0] + buf_b[1]) + (buf_b[2] + buf_b[3])

    cell = y * 4 + k4
    one_a[cell] = jnp.zeros_like(one_a[cell])
    two_a[cell] = jnp.zeros_like(two_a[cell])
    part[0, tail, :] = jnp.zeros((tail.size, LANES), F32)
    part[1, tail, :] = jnp.zeros((tail.size, LANES), F32)

    def after(p):
        done = []
        for h in order[1:]:
            last = block_of(h).start + HEAD_DIM - 1
            if min(last // PIECE, PIECES - 1) == p:
                done.append(h)
        return done

    pieces = range(PIECES)
    A = [p for p in pieces if KINDS[p] == "a"]
    B = [p for p in pieces if KINDS[p] == "b"]

    def state_blocks(p, spread):
        for h in ([SPLIT_HEAD] if p == 0 else []) + ready[p]:
            block = dot(feat_k[rows_of(h), :], pad(v_in[rows_of(h), :]), NT)
            if h == SPLIT_HEAD:
                spread = block
            else:
                place(0, h, block, spread)
        return spread

    ready = []
    for p in pieces:
        ready.append(
            [
                h
                for h in order[1:]
                if (p - 1 if p else -1) * PIECE + PIECE <= block_of(h).start < (p + 1) * PIECE
            ]
        )

    for load in loads[:3]:
        load.wait()
    gain_row[...] = jnp.ones_like(gain_row)
    for h in range(HEADS):
        cut = pl.ds(h * HEAD_DIM, HEAD_DIM)
        gain_row[h, 0:HEAD_DIM] = qg_ref[cut]
        gain_row[16 + h, 0:HEAD_DIM] = kg_ref[cut]
    gain_col[...] = jnp.transpose(gain_row[...])
    for h in range(HEADS):
        feat = features(k_in, inv_k, k_gain, feat_k, h)
        one_a[cell, h : h + 1, 0:HEAD_DIM] = dot(ones, feat, NT)[0:1]
    pl.semaphore_wait(barrier, greeted)
    pl.semaphore_signal(far_sem, inc=1, device_id=at(0, 4), device_id_type=MESH)
    ar1 = small_cluster(0, one_a)
    loads[3].wait()
    spread = None
    for p in pieces:
        spread = state_blocks(p, spread)
        step(0, p)
    loads[4].wait()
    for h in range(HEADS):
        features(q_in, inv_q, q_gain, feat_q, h)
    pl.semaphore_wait(far_sem, 1)
    ar1 = small_stride(1, ar1, one_a, one_b)
    step(0, *A, *B, *A)

    loads[5].wait()
    key_total = small_done(ar1, one_b)
    kt_col[...] = jnp.transpose(key_total)
    kt_hi, kt_mid = split(key_total)
    kt_lo = (key_total - kt_hi.astype(F32) - kt_mid.astype(F32)).astype(BF16)
    kt3 = jnp.concatenate([kt_hi, kt_mid, kt_lo], axis=0)[:, 0:HEAD_DIM]
    loss_scale = math.sqrt(clip_tokens)

    def grad_state_blocks(p, spread):
        for h in ([SPLIT_HEAD] if p == 0 else []) + ready[p]:
            feat = feat_q[rows_of(h), :]
            terms = dot(kt3, feat, NN)
            denominator = (
                terms[h : h + 1] + (terms[16 + h : 17 + h] + terms[32 + h : 33 + h])
            ) + denom_eps
            inverse = 1.0 / denominator
            rden[h : h + 1, :] = inverse
            scaled = g_in[rows_of(h), :].astype(F32) * (loss_scale * inverse)
            high, low = split(scaled)
            scaled_hi[rows_of(h), :] = high
            scaled_lo[rows_of(h), :] = low
            block = dot(feat, pad(high), NT) + dot(feat, pad(low), NT)
            if h == SPLIT_HEAD:
                spread = block
            else:
                place(1, h, block, spread)
        return spread

    for p in pieces:
        spread = grad_state_blocks(p, spread)
        step(1, p)
    step(1, *A)
    step(0, *B, *A)
    step(1, *B, *A)
    step(0, *B, *A, *A)

    def query_head(h):
        feat = feat_q[rows_of(h), :]
        high, low = scaled_hi[rows_of(h), :], scaled_lo[rows_of(h), :]
        state_hi, state_lo = split(take(0, h))
        grad = dot(state_hi, high, NN) + (dot(state_lo, high, NN) + dot(state_hi, low, NN))
        feat_f = feat.astype(F32)
        projected = jnp.sum(feat_f * grad, axis=0, keepdims=True) * rden[h : h + 1, :]
        grad = grad - kt_col[0:HEAD_DIM, h : h + 1] * projected
        grad_f[rows_of(h), :] = grad
        p_hi, p_lo = split(-projected)
        two_a[cell, HEADS + h : HEADS + h + 1, 0:HEAD_DIM] = (
            dot(jnp.broadcast_to(p_hi, (16, tokens)), feat, NT)
            + dot(jnp.broadcast_to(p_lo, (16, tokens)), feat, NT)
        )[0:1]
        e_hi, e_lo = split(feat_f * grad)
        two_a[cell, h : h + 1, 0:HEAD_DIM] = (
            dot(ones, e_hi, NT) + dot(ones, e_lo, NT)
        )[0:1]

    arrives = [[h for h in after(p)] for p in pieces]
    arrives[-1].append(SPLIT_HEAD)

    for p in pieces:
        step(0, p)
        for h in arrives[p]:
            query_head(h)
    ar2 = small_cluster(2, two_a)
    step(1, *A, *B)

    def norm_backward(x_in, inv_ref, gain, feat, grad, out, h):
        inverse = inv_ref[h : h + 1, :]
        unit = x_in[rows_of(h), :].astype(F32) * inverse
        upstream = jnp.where(feat > 0, grad, 0.0) * gain(h)
        mean = jnp.sum(upstream * unit, axis=0, keepdims=True) * (1.0 / HEAD_DIM)
        out[rows_of(h), :] = (inverse * (upstream - unit * mean)).astype(BF16)

    def grad_queries(heads):
        for h in heads:
            feat = feat_q[rows_of(h), :].astype(F32)
            norm_backward(q_in, inv_q, q_gain, feat, grad_f[rows_of(h), :], out_q, h)

    grad_queries(range(0, 5))
    ar2 = small_stride(3, ar2, two_a, two_b)
    step(1, *A, *B)
    grad_queries(range(5, HEADS))
    store_q = pltpu.make_async_copy(out_q, gq_hbm.at[0], store_sem.at[0])
    store_q.start()
    step(1, *A)

    total = small_done(ar2, two_b)
    three[dp] = total[0:16]
    ref = three.at[dp]
    ar3 = go(
        small_recv.at[4], [(ref, ref, (lax.rem(dp + r, dps), space)) for r in range(1, dps)]
    )

    for p in pieces:
        step(1, p)
        for h in arrives[p]:
            gs_hi, gs_lo = split(take(1, h))
            value = v_in[rows_of(h), :]
            feat = feat_k[rows_of(h), :]
            out_v[rows_of(h), :] = (dot(gs_hi, feat, TN) + dot(gs_lo, feat, TN)).astype(BF16)
            grad_f[rows_of(h), :] = dot(gs_hi, value, NN) + dot(gs_lo, value, NN)
    store_v = pltpu.make_async_copy(out_v, gv_hbm.at[0], store_sem.at[1])
    store_v.start()

    gkt_col = jnp.transpose(total)
    for h in range(HEADS):
        feat = feat_k[rows_of(h), :].astype(F32)
        grad = grad_f[rows_of(h), :] + gkt_col[0:HEAD_DIM, HEADS + h : HEADS + h + 1]
        norm_backward(k_in, inv_k, k_gain, feat, grad, out_k, h)
    store_k = pltpu.make_async_copy(out_k, gk_hbm.at[0], store_sem.at[2])
    store_k.start()

    land(ar3)
    total = three[0]
    for r in range(1, dps):
        total = total + three[r]
    gain_sum = total[0:HEADS, 0:HEAD_DIM] * (1.0 / math.sqrt(all_rows))
    grad_q_gain = gain_sum / gain_row[0:HEADS, 0:HEAD_DIM]
    grad_k_gain = gain_sum / gain_row[16 : 16 + HEADS, 0:HEAD_DIM]
    for h in range(HEADS):
        cut = pl.ds(h * HEAD_DIM, HEAD_DIM)
        gain_q_out[cut] = grad_q_gain[h]
        gain_k_out[cut] = grad_k_gain[h]
    store_gains = [
        pltpu.make_async_copy(gain_q_out, gain_q_hbm, store_sem.at[3]),
        pltpu.make_async_copy(gain_k_out, gain_k_hbm, store_sem.at[4]),
    ]
    for store in store_gains:
        store.start()

    wait_rows(send_sem, sent[0])
    for store in (store_q, store_v, store_k, *store_gains):
        store.wait()


def hand_over(*refs):
    sources, results, held, load_sem, store_sem = refs[:3], refs[3:6], *refs[6:]
    rows = CH // CUTS
    loads, stores = [], []
    for i, (src, dst) in enumerate(zip(sources, results)):
        for part in range(CUTS):
            cut = pl.ds(part * rows, rows)
            n = i * CUTS + part
            loads.append(pltpu.make_async_copy(src.at[0, cut], held.at[i, cut], load_sem.at[n]))
            stores.append(pltpu.make_async_copy(held.at[i, cut], dst.at[0, cut], store_sem.at[n]))
    for load in loads:
        load.start()
    for load, store in zip(loads, stores):
        load.wait()
        store.start()
    for store in stores:
        store.wait()


def local(queries, keys, values, out_grad, q_gain, k_gain):
    tokens = queries.shape[2]
    dps = lax.axis_size("dp")
    clip_tokens = tokens * lax.axis_size("space")
    all_rows = clip_tokens * dps * queries.shape[0]
    anywhere = pl.BlockSpec(memory_space=pl.ANY)
    big = jax.ShapeDtypeStruct(queries.shape, BF16)
    row = jax.ShapeDtypeStruct((CH,), F32)
    vm = pltpu.VMEM
    dma = pltpu.SemaphoreType.DMA

    def run(*refs):
        kernel(clip_tokens, all_rows, dps, *refs)

    *grads, gain_q, gain_k = pl.pallas_call(
        run,
        out_shape=(big, big, big, row, row),
        in_specs=[anywhere] * 6,
        out_specs=(anywhere,) * 5,
        scratch_shapes=[
            vm((CH, tokens), BF16),
            vm((CH, tokens), BF16),
            vm((CH, tokens), BF16),
            vm((CH, tokens), BF16),
            vm((CH,), F32),
            vm((CH,), F32),
            vm((CH,), F32),
            vm((CH,), F32),
            vm((CH, tokens), BF16),
            vm((CH, tokens), BF16),
            vm((16, tokens), F32),
            vm((16, tokens), F32),
            vm((16, tokens), F32),
            vm((CH, tokens), BF16),
            vm((CH, tokens), BF16),
            vm((CH, tokens), F32),
            vm((CH, tokens), BF16),
            vm((CH, tokens), BF16),
            vm((CH, tokens), BF16),
            vm((32, LANES), F32),
            vm((LANES, 32), F32),
            vm((LANES, 16), F32),
            vm((2, ROWS, LANES), F32),
            vm((2, PIECES, HALF, LANES), F32),
            vm((2, PIECES, HALF, LANES), F32),
            vm((2, PIECES, 3, CLASS, LANES), F32),
            vm((2, PIECES, CLASS, LANES), F32),
            vm((2, PIECES, 7, OWN, LANES), F32),
            vm((2, ROWS, LANES), F32),
            vm((8, 16, LANES), F32),
            vm((4, 16, LANES), F32),
            vm((8, 24, LANES), F32),
            vm((4, 24, LANES), F32),
            vm((dps, 16, LANES), F32),
            vm((2 * 2048 + 640, LANES), F32),
            dma((6,)),
            dma((5,)),
            dma(()),
            dma((2, PIECES, STAGES)),
            dma((5,)),
            pltpu.SemaphoreType.REGULAR,
        ],
        compiler_params=pltpu.CompilerParams(
            collective_id=0, has_side_effects=True, vmem_limit_bytes=VMEM_BYTES
        ),
        name="linear_attention_backward",
    )(queries, keys, values, out_grad, q_gain, k_gain)
    grads = pl.pallas_call(
        hand_over,
        out_shape=(big, big, big),
        in_specs=[anywhere] * 3,
        out_specs=(anywhere,) * 3,
        scratch_shapes=[vm((3, CH, tokens), BF16), dma((3 * CUTS,)), dma((3 * CUTS,))],
        compiler_params=pltpu.CompilerParams(vmem_limit_bytes=VMEM_BYTES),
        name="hand_over",
    )(*grads)
    return (*grads, gain_q, gain_k)


def solution(mesh):
    whole = P("dp", None, "space")
    return jax.shard_map(
        local,
        mesh=mesh,
        in_specs=(whole, whole, whole, whole, P(), P()),
        out_specs=(whole, whole, whole, P(), P()),
        check_vma=False,
    )
```

```python
import math

import jax
import jax.numpy as jnp
from jax import lax
from jax.experimental import pallas as pl
from jax.experimental.pallas import tpu as pltpu
from jax.sharding import PartitionSpec as P

HEADS = 10
HEAD_DIM = 112
CH = HEADS * HEAD_DIM
LANES = 128
SPLIT_HEAD = 7
SPARE = LANES - HEAD_DIM
HOSTS = HEAD_DIM // SPARE
ROWS = 1024
PIECES = 4
PIECE = ROWS // PIECES
HALF = PIECE // 2
OWN = HALF // 16
STAGES = 6
SPOTS = (-1, -3, -6, 1, 3, 6, -2, -4, -7, -5, -8, 2, 4, 7, 5, 0)
COLLECT = 6
STAGE_AT = (0.0, 3.0, 6.2, 11.7, 17.0, 20.0, 23.2)
PIECE_GAP = 1.3
GRAD_LAG = 10.4
OPPOSITE = (3, 4, 5, 0, 1, 2)
HANDS = ((-1, 6, 9, 0), (-2, 9, 11, 1), (1, 11, 14, 3), (2, 14, 15, 4))
VMEM_BYTES = 62 << 20
CUTS = 2
Y, Z = 2, 16

norm_eps = 1e-06
denom_eps = 1e-06
F32 = jnp.float32
BF16 = jnp.bfloat16
MESH = pl.DeviceIdType.MESH
NT = (((1,), (1,)), ((), ()))
NN = (((1,), (0,)), ((), ()))
TN = (((0,), (0,)), ((), ()))


def dot(a, b, dims):
    return lax.dot_general(a, b, dims, preferred_element_type=F32)


def split(x):
    high = x.astype(BF16)
    return high, (x - high.astype(F32)).astype(BF16)


def rows_of(head):
    return pl.ds(head * HEAD_DIM, HEAD_DIM)


def block_of(head):
    return pl.ds((head if head < SPLIT_HEAD else head - 1) * HEAD_DIM, HEAD_DIM)


def kernel(
    clip_tokens,
    all_rows,
    dps,
    q_hbm,
    k_hbm,
    v_hbm,
    g_hbm,
    qg_hbm,
    kg_hbm,
    gq_hbm,
    gk_hbm,
    gv_hbm,
    gain_q_hbm,
    gain_k_hbm,
    q_in,
    k_in,
    v_in,
    g_in,
    qg_ref,
    kg_ref,
    gain_q_out,
    gain_k_out,
    feat_q,
    feat_k,
    inv_q,
    inv_k,
    rden,
    scaled_hi,
    scaled_lo,
    grad_f,
    out_q,
    out_k,
    out_v,
    gain_row,
    gain_col,
    kt_col,
    part,
    recv_y,
    half,
    recv_w,
    recv_s,
    held,
    full,
    one_a,
    one_b,
    two_a,
    two_b,
    three,
    sizes,
    load_sem,
    store_sem,
    send_sem,
    big_recv,
    small_recv,
    far_sem,
):
    tokens = q_in.shape[1]
    dp = lax.axis_index("dp")
    space = lax.axis_index("space")
    y, z = space // Z, space % Z
    k4, g4 = z % 4, z // 4
    sign = 1 - 2 * (dp % 2)

    def at(dy, dz):
        return (dp, lax.rem(y + dy, Y) * Z + lax.rem(z + dz + 2 * Z, Z))

    loads = [
        pltpu.make_async_copy(src, dst, load_sem.at[i])
        for i, (src, dst) in enumerate(
            (
                (k_hbm.at[0], k_in),
                (kg_hbm, kg_ref),
                (qg_hbm, qg_ref),
                (v_hbm.at[0], v_in),
                (q_hbm.at[0], q_in),
                (g_hbm.at[0], g_in),
            )
        )
    ]
    for load in loads:
        load.start()

    barrier = pltpu.get_barrier_semaphore()

    def cluster_peer(r):
        return (dp, lax.rem(y + r // 4, Y) * Z + g4 * 4 + lax.rem(k4 + r % 4, 4))

    greeted = 0
    for r in range(1, 8):
        pl.semaphore_signal(barrier, inc=1, device_id=cluster_peer(r), device_id_type=MESH)
        greeted += 1
    for dy, dz in ((0, 1), (0, -1), (0, 2), (0, -2), (0, 3), (0, -3), (0, 4), (0, -4)):
        pl.semaphore_signal(barrier, inc=1, device_id=at(dy, dz), device_id_type=MESH)
        greeted += 1
    for r in range(1, dps):
        pl.semaphore_signal(
            barrier, inc=1, device_id=(lax.rem(dp + r, dps), space), device_id_type=MESH
        )
        greeted += 1

    lane = lax.broadcasted_iota(jnp.int32, (HEAD_DIM, LANES), 1)
    ones = jnp.ones((16, tokens), BF16)
    no_rows = jnp.zeros((SPARE, tokens), BF16)

    def q_gain(h):
        return gain_col[0:HEAD_DIM, h : h + 1]

    def k_gain(h):
        return gain_col[0:HEAD_DIM, 16 + h : 17 + h]

    def pad(x):
        return jnp.concatenate([x, no_rows], axis=0)

    def features(x_in, inv_ref, gain, feat_ref, h):
        x = x_in[rows_of(h), :].astype(F32)
        inverse = lax.rsqrt(jnp.sum(x * x, axis=0, keepdims=True) * (1.0 / HEAD_DIM) + norm_eps)
        inv_ref[h : h + 1, :] = inverse
        feat = jnp.maximum((x * inverse) * gain(h), 0.0).astype(BF16)
        feat_ref[rows_of(h), :] = feat
        return feat

    def place(a, h, block, spread):
        if h < HOSTS:
            moved = pltpu.roll(spread, (HEAD_DIM - SPARE * h) % LANES, 1)
            block = jnp.where(lane >= HEAD_DIM, moved, block)
        part[a, block_of(h), :] = block

    def take(a, h):
        if h != SPLIT_HEAD:
            return full[a, block_of(h), :][:, 0:HEAD_DIM]
        whole = jnp.zeros((HEAD_DIM, LANES), F32)
        for j in range(HOSTS):
            moved = pltpu.roll(full[a, block_of(j), :], (SPARE * j - HEAD_DIM) % LANES, 1)
            whole = jnp.where((lane >= SPARE * j) & (lane < SPARE * (j + 1)), moved, whole)
        return whole[:, 0:HEAD_DIM]

    order = [SPLIT_HEAD] + [h for h in range(HEADS) if h != SPLIT_HEAD]
    tail = pl.ds((HEADS - 1) * HEAD_DIM, ROWS - (HEADS - 1) * HEAD_DIM)

    sent = [0]

    def go(recv_sem, copies):
        rows = 0
        for src, dst, peer in copies:
            pltpu.make_async_remote_copy(
                src_ref=src,
                dst_ref=dst,
                send_sem=send_sem,
                recv_sem=recv_sem,
                device_id=peer,
                device_id_type=MESH,
            ).start()
            rows += src.shape[0]
        sent[0] += rows
        return recv_sem, rows

    def wait_rows(sem, rows):
        ref = sizes.at[pl.ds(0, rows)]
        pltpu.make_async_copy(ref, ref, sem).wait()

    def land(came):
        wait_rows(*came)

    stride = (4, 12, 8)

    def near(start, size):
        return pl.ds(pl.multiple_of(start, size), size)

    def owner_rows(spot):
        return lax.rem(z + SPOTS[spot] * sign + Z, Z) * OWN

    def spots(first, last):
        return pl.ds(first * OWN, (last - first) * OWN)

    def rs_y(a, p, came):
        src = part.at[a, near(p * PIECE + lax.rem(y + 1, Y) * HALF, HALF)]
        return go(big_recv.at[a, p, 0], [(src, recv_y.at[a, p], at(1, 0))])

    def rs_w(a, p, came):
        land(came)
        base = p * PIECE + y * HALF
        for spot in range(16):
            rows = owner_rows(spot)
            half[a, p, pl.ds(spot * OWN, OWN), :] = (
                part[a, near(base + rows, OWN), :] + recv_y[a, p, near(rows, OWN), :]
            )
        copies, filled = [], 0
        for dz, first, last, _ in HANDS:
            dst = recv_w.at[a, p, spots(filled, filled + last - first)]
            copies.append((half.at[a, p, spots(first, last)], dst, at(0, dz * sign)))
            filled += last - first
        return go(big_recv.at[a, p, 1], copies)

    def rs_s(a, p, came):
        land(came)
        filled = 0
        for dz, first, last, to in HANDS:
            count = last - first
            mine = spots(to, to + count)
            half[a, p, mine, :] = half[a, p, mine, :] + recv_w[a, p, spots(filled, filled + count), :]
            filled += count
        return go(
            big_recv.at[a, p, 2],
            [
                (half.at[a, p, spots(i, i + 1)], recv_s.at[a, p, i], at(0, SPOTS[i] * sign))
                for i in range(COLLECT)
            ],
        )

    def ag_s(a, p, came):
        land(came)
        own = spots(15, 16)
        total = half[a, p, own, :]
        for i in range(COLLECT):
            total = total + recv_s[a, p, i]
        held[a, p, 0, own, :] = total
        return go(
            big_recv.at[a, p, 3],
            [
                (held.at[a, p, 0, own], held.at[a, p, 0, spots(OPPOSITE[i], OPPOSITE[i] + 1)], at(0, SPOTS[i] * sign))
                for i in range(COLLECT)
            ],
        )

    def ag_w(a, p, came):
        land(came)
        copies = []
        for dz, first, last, to in HANDS:
            src = held.at[a, p, 0, spots(to, to + last - first)]
            copies.append((src, held.at[a, p, 0, spots(first, last)], at(0, -dz * sign)))
        return go(big_recv.at[a, p, 4], copies)

    def ag_y(a, p, came):
        land(came)
        came = go(big_recv.at[a, p, 5], [(held.at[a, p, 0], held.at[a, p, 1], at(1, 0))])
        spread_out(a, p, 0, y)
        return came

    def spread_out(a, p, which, side):
        for spot in range(16):
            rows = near(p * PIECE + side * HALF + owner_rows(spot), OWN)
            full[a, rows, :] = held[a, p, which, pl.ds(spot * OWN, OWN), :]

    todo = (rs_y, rs_w, rs_s, ag_s, ag_w, ag_y)
    under_way = {}

    def step(a, *pieces):
        for p in pieces:
            at_stage, came = under_way.get((a, p), (0, None))
            if at_stage < len(todo):
                came = todo[at_stage](a, p, came)
            else:
                land(came)
                spread_out(a, p, 1, lax.rem(y + 1, Y))
            under_way[a, p] = (at_stage + 1, came)

    def small_cluster(slot, buf):
        ref = buf.at[y * 4 + k4]
        return go(small_recv.at[slot], [(ref, ref, cluster_peer(r)) for r in range(1, 8)])

    def small_stride(slot, came, buf_a, buf_b):
        land(came)
        total = buf_a[0]
        for e in range(1, 8):
            total = total + buf_a[e]
        buf_b[g4] = total
        ref = buf_b.at[g4]
        return go(small_recv.at[slot], [(ref, ref, at(0, dz)) for dz in stride])

    def small_done(came, buf_b):
        land(came)
        return (buf_b[0] + buf_b[1]) + (buf_b[2] + buf_b[3])

    cell = y * 4 + k4
    one_a[cell] = jnp.zeros_like(one_a[cell])
    two_a[cell] = jnp.zeros_like(two_a[cell])
    part[0, tail, :] = jnp.zeros((tail.size, LANES), F32)
    part[1, tail, :] = jnp.zeros((tail.size, LANES), F32)

    def after(p):
        done = []
        for h in order[1:]:
            last = block_of(h).start + HEAD_DIM - 1
            if min(last // PIECE, PIECES - 1) == p:
                done.append(h)
        return done

    pieces = range(PIECES)
    A = list(pieces)
    B = []

    def state_blocks(p, spread):
        for h in ([SPLIT_HEAD] if p == 0 else []) + ready[p]:
            block = dot(feat_k[rows_of(h), :], pad(v_in[rows_of(h), :]), NT)
            if h == SPLIT_HEAD:
                spread = block
            else:
                place(0, h, block, spread)
        return spread

    ready = []
    for p in pieces:
        ready.append(
            [
                h
                for h in order[1:]
                if (p - 1 if p else -1) * PIECE + PIECE <= block_of(h).start < (p + 1) * PIECE
            ]
        )

    for load in loads[:3]:
        load.wait()
    gain_row[...] = jnp.ones_like(gain_row)
    for h in range(HEADS):
        cut = pl.ds(h * HEAD_DIM, HEAD_DIM)
        gain_row[h, 0:HEAD_DIM] = qg_ref[cut]
        gain_row[16 + h, 0:HEAD_DIM] = kg_ref[cut]
    gain_col[...] = jnp.transpose(gain_row[...])
    for h in range(HEADS):
        feat = features(k_in, inv_k, k_gain, feat_k, h)
        one_a[cell, h : h + 1, 0:HEAD_DIM] = dot(ones, feat, NT)[0:1]
    pl.semaphore_wait(barrier, greeted)
    for dz in (4, -4):
        pl.semaphore_signal(far_sem, inc=1, device_id=at(0, dz), device_id_type=MESH)
    ar1 = small_cluster(0, one_a)
    loads[3].wait()
    spread = None
    for p in pieces:
        spread = state_blocks(p, spread)
        step(0, p)
    loads[4].wait()
    for h in range(HEADS):
        features(q_in, inv_q, q_gain, feat_q, h)
    step(0, 0)
    pl.semaphore_wait(far_sem, 2)
    ar1 = small_stride(1, ar1, one_a, one_b)
    step(0, 1, 2, 3, 0, 1, 2, 3)

    loads[5].wait()
    key_total = small_done(ar1, one_b)
    kt_col[...] = jnp.transpose(key_total)
    kt_hi, kt_mid = split(key_total)
    kt_lo = (key_total - kt_hi.astype(F32) - kt_mid.astype(F32)).astype(BF16)
    kt3 = jnp.concatenate([kt_hi, kt_mid, kt_lo], axis=0)[:, 0:HEAD_DIM]
    loss_scale = math.sqrt(clip_tokens)

    def grad_state_blocks(p, spread):
        for h in ([SPLIT_HEAD] if p == 0 else []) + ready[p]:
            feat = feat_q[rows_of(h), :]
            terms = dot(kt3, feat, NN)
            denominator = (
                terms[h : h + 1] + (terms[16 + h : 17 + h] + terms[32 + h : 33 + h])
            ) + denom_eps
            inverse = 1.0 / denominator
            rden[h : h + 1, :] = inverse
            scaled = g_in[rows_of(h), :].astype(F32) * (loss_scale * inverse)
            high, low = split(scaled)
            scaled_hi[rows_of(h), :] = high
            scaled_lo[rows_of(h), :] = low
            block = dot(feat, pad(high), NT) + dot(feat, pad(low), NT)
            if h == SPLIT_HEAD:
                spread = block
            else:
                place(1, h, block, spread)
        return spread

    for p in pieces:
        spread = grad_state_blocks(p, spread)
        step(1, p)

    def query_head(h):
        feat = feat_q[rows_of(h), :]
        high, low = scaled_hi[rows_of(h), :], scaled_lo[rows_of(h), :]
        state_hi, state_lo = split(take(0, h))
        grad = dot(state_hi, high, NN) + (dot(state_lo, high, NN) + dot(state_hi, low, NN))
        feat_f = feat.astype(F32)
        projected = jnp.sum(feat_f * grad, axis=0, keepdims=True) * rden[h : h + 1, :]
        grad = grad - kt_col[0:HEAD_DIM, h : h + 1] * projected
        grad_f[rows_of(h), :] = grad
        p_hi, p_lo = split(-projected)
        two_a[cell, HEADS + h : HEADS + h + 1, 0:HEAD_DIM] = (
            dot(jnp.broadcast_to(p_hi, (16, tokens)), feat, NT)
            + dot(jnp.broadcast_to(p_lo, (16, tokens)), feat, NT)
        )[0:1]
        e_hi, e_lo = split(feat_f * grad)
        two_a[cell, h : h + 1, 0:HEAD_DIM] = (
            dot(ones, e_hi, NT) + dot(ones, e_lo, NT)
        )[0:1]

    arrives = [[h for h in after(p)] for p in pieces]
    arrives[-1].append(SPLIT_HEAD)

    last = len(todo)
    order_of_steps = sorted(
        (STAGE_AT[k] + PIECE_GAP * p + GRAD_LAG * a, a, p, k)
        for a, first in ((0, 3), (1, 1))
        for p in pieces
        for k in range(first, last + 1)
    )
    end = order_of_steps.index((STAGE_AT[last] + PIECE_GAP * (PIECES - 1), 0, PIECES - 1, last))
    for _, a, p, k in order_of_steps[: end + 1]:
        step(a, p)
        if a == 0 and k == last:
            for h in arrives[p]:
                query_head(h)
    ar2 = small_cluster(2, two_a)

    def norm_backward(x_in, inv_ref, gain, feat, grad, out, h):
        inverse = inv_ref[h : h + 1, :]
        unit = x_in[rows_of(h), :].astype(F32) * inverse
        upstream = jnp.where(feat > 0, grad, 0.0) * gain(h)
        mean = jnp.sum(upstream * unit, axis=0, keepdims=True) * (1.0 / HEAD_DIM)
        out[rows_of(h), :] = (inverse * (upstream - unit * mean)).astype(BF16)

    def grad_queries(heads):
        for h in heads:
            feat = feat_q[rows_of(h), :].astype(F32)
            norm_backward(q_in, inv_q, q_gain, feat, grad_f[rows_of(h), :], out_q, h)

    rest = [(p, k) for _, a, p, k in order_of_steps[end + 1 :]]

    def go_on(stage):
        for p, k in rest:
            if k == stage:
                step(1, p)

    go_on(3)
    grad_queries(range(0, 5))
    go_on(4)
    ar2 = small_stride(3, ar2, two_a, two_b)
    grad_queries(range(5, HEADS))
    store_q = pltpu.make_async_copy(out_q, gq_hbm.at[0], store_sem.at[0])
    store_q.start()
    go_on(5)

    for p in pieces:
        step(1, p)
        for h in arrives[p]:
            gs_hi, gs_lo = split(take(1, h))
            value = v_in[rows_of(h), :]
            feat = feat_k[rows_of(h), :]
            out_v[rows_of(h), :] = (dot(gs_hi, feat, TN) + dot(gs_lo, feat, TN)).astype(BF16)
            grad_f[rows_of(h), :] = dot(gs_hi, value, NN) + dot(gs_lo, value, NN)
    store_v = pltpu.make_async_copy(out_v, gv_hbm.at[0], store_sem.at[1])
    store_v.start()

    total = small_done(ar2, two_b)
    three[dp] = total[0:16]
    ref = three.at[dp]
    ar3 = go(
        small_recv.at[4], [(ref, ref, (lax.rem(dp + r, dps), space)) for r in range(1, dps)]
    )

    gkt_col = jnp.transpose(total)
    for h in range(HEADS):
        feat = feat_k[rows_of(h), :].astype(F32)
        grad = grad_f[rows_of(h), :] + gkt_col[0:HEAD_DIM, HEADS + h : HEADS + h + 1]
        norm_backward(k_in, inv_k, k_gain, feat, grad, out_k, h)
    store_k = pltpu.make_async_copy(out_k, gk_hbm.at[0], store_sem.at[2])
    store_k.start()

    land(ar3)
    total = three[0]
    for r in range(1, dps):
        total = total + three[r]
    gain_sum = total[0:HEADS, 0:HEAD_DIM] * (1.0 / math.sqrt(all_rows))
    grad_q_gain = gain_sum / gain_row[0:HEADS, 0:HEAD_DIM]
    grad_k_gain = gain_sum / gain_row[16 : 16 + HEADS, 0:HEAD_DIM]
    for h in range(HEADS):
        cut = pl.ds(h * HEAD_DIM, HEAD_DIM)
        gain_q_out[cut] = grad_q_gain[h]
        gain_k_out[cut] = grad_k_gain[h]
    store_gains = [
        pltpu.make_async_copy(gain_q_out, gain_q_hbm, store_sem.at[3]),
        pltpu.make_async_copy(gain_k_out, gain_k_hbm, store_sem.at[4]),
    ]
    for store in store_gains:
        store.start()

    wait_rows(send_sem, sent[0])
    for store in (store_q, store_v, store_k, *store_gains):
        store.wait()


def hand_over(*refs):
    sources, results, held, load_sem, store_sem = refs[:3], refs[3:6], *refs[6:]
    rows = CH // CUTS
    loads, stores = [], []
    for i, (src, dst) in enumerate(zip(sources, results)):
        for part in range(CUTS):
            cut = pl.ds(part * rows, rows)
            n = i * CUTS + part
            loads.append(pltpu.make_async_copy(src.at[0, cut], held.at[i, cut], load_sem.at[n]))
            stores.append(pltpu.make_async_copy(held.at[i, cut], dst.at[0, cut], store_sem.at[n]))
    for load in loads:
        load.start()
    for load, store in zip(loads, stores):
        load.wait()
        store.start()
    for store in stores:
        store.wait()


def local(queries, keys, values, out_grad, q_gain, k_gain):
    tokens = queries.shape[2]
    dps = lax.axis_size("dp")
    clip_tokens = tokens * lax.axis_size("space")
    all_rows = clip_tokens * dps * queries.shape[0]
    anywhere = pl.BlockSpec(memory_space=pl.ANY)
    big = jax.ShapeDtypeStruct(queries.shape, BF16)
    row = jax.ShapeDtypeStruct((CH,), F32)
    vm = pltpu.VMEM
    dma = pltpu.SemaphoreType.DMA

    def run(*refs):
        kernel(clip_tokens, all_rows, dps, *refs)

    *grads, gain_q, gain_k = pl.pallas_call(
        run,
        out_shape=(big, big, big, row, row),
        in_specs=[anywhere] * 6,
        out_specs=(anywhere,) * 5,
        scratch_shapes=[
            vm((CH, tokens), BF16),
            vm((CH, tokens), BF16),
            vm((CH, tokens), BF16),
            vm((CH, tokens), BF16),
            vm((CH,), F32),
            vm((CH,), F32),
            vm((CH,), F32),
            vm((CH,), F32),
            vm((CH, tokens), BF16),
            vm((CH, tokens), BF16),
            vm((16, tokens), F32),
            vm((16, tokens), F32),
            vm((16, tokens), F32),
            vm((CH, tokens), BF16),
            vm((CH, tokens), BF16),
            vm((CH, tokens), F32),
            vm((CH, tokens), BF16),
            vm((CH, tokens), BF16),
            vm((CH, tokens), BF16),
            vm((32, LANES), F32),
            vm((LANES, 32), F32),
            vm((LANES, 16), F32),
            vm((2, ROWS, LANES), F32),
            vm((2, PIECES, HALF, LANES), F32),
            vm((2, PIECES, HALF, LANES), F32),
            vm((2, PIECES, 9 * OWN, LANES), F32),
            vm((2, PIECES, COLLECT, OWN, LANES), F32),
            vm((2, PIECES, 2, HALF, LANES), F32),
            vm((2, ROWS, LANES), F32),
            vm((8, 16, LANES), F32),
            vm((4, 16, LANES), F32),
            vm((8, 24, LANES), F32),
            vm((4, 24, LANES), F32),
            vm((dps, 16, LANES), F32),
            vm((2 * 2048 + 640, LANES), F32),
            dma((6,)),
            dma((5,)),
            dma(()),
            dma((2, PIECES, STAGES)),
            dma((5,)),
            pltpu.SemaphoreType.REGULAR,
        ],
        compiler_params=pltpu.CompilerParams(
            collective_id=0, has_side_effects=True, vmem_limit_bytes=VMEM_BYTES
        ),
        name="linear_attention_backward",
    )(queries, keys, values, out_grad, q_gain, k_gain)
    grads = pl.pallas_call(
        hand_over,
        out_shape=(big, big, big),
        in_specs=[anywhere] * 3,
        out_specs=(anywhere,) * 3,
        scratch_shapes=[vm((3, CH, tokens), BF16), dma((3 * CUTS,)), dma((3 * CUTS,))],
        compiler_params=pltpu.CompilerParams(vmem_limit_bytes=VMEM_BYTES),
        name="hand_over",
    )(*grads)
    return (*grads, gain_q, gain_k)


def solution(mesh):
    whole = P("dp", None, "space")
    return jax.shard_map(
        local,
        mesh=mesh,
        in_specs=(whole, whole, whole, whole, P(), P()),
        out_specs=(whole, whole, whole, P(), P()),
        check_vma=False,
    )
```

```python
import math

import jax
import jax.numpy as jnp
from jax import lax
from jax.experimental import pallas as pl
from jax.experimental.pallas import tpu as pltpu
from jax.sharding import PartitionSpec as P

HEADS = 10
HEAD_DIM = 112
CH = HEADS * HEAD_DIM
LANES = 128
SPLIT_HEAD = 7
SPARE = LANES - HEAD_DIM
HOSTS = HEAD_DIM // SPARE
ROWS = 1024
PIECES = 4
PIECE = ROWS // PIECES
HALF = PIECE // 2
OWN = HALF // 16
STAGES = 6
SPOTS = (-1, -3, -6, 1, 3, 6, -2, -4, -7, -5, -8, 2, 4, 7, 5, 0)
COLLECT = 6
STAGE_AT = (0.0, 3.0, 6.2, 11.7, 17.0, 20.0, 23.2)
PIECE_GAP = 0.9
GRAD_LAG = 10.4
OPPOSITE = (3, 4, 5, 0, 1, 2)
HANDS = ((-1, 6, 9, 0), (-2, 9, 11, 1), (1, 11, 14, 3), (2, 14, 15, 4))
VMEM_BYTES = 62 << 20
Y, Z = 2, 16

norm_eps = 1e-06
denom_eps = 1e-06
F32 = jnp.float32
BF16 = jnp.bfloat16
MESH = pl.DeviceIdType.MESH
NT = (((1,), (1,)), ((), ()))
NN = (((1,), (0,)), ((), ()))
TN = (((0,), (0,)), ((), ()))


def dot(a, b, dims):
    return lax.dot_general(a, b, dims, preferred_element_type=F32)


def split(x):
    high = x.astype(BF16)
    return high, (x - high.astype(F32)).astype(BF16)


def rows_of(head):
    return pl.ds(head * HEAD_DIM, HEAD_DIM)


def block_of(head):
    return pl.ds((head if head < SPLIT_HEAD else head - 1) * HEAD_DIM, HEAD_DIM)


def kernel(
    clip_tokens,
    all_rows,
    dps,
    q_hbm,
    k_hbm,
    v_hbm,
    g_hbm,
    qg_hbm,
    kg_hbm,
    out_q,
    out_k,
    out_v,
    gain_q_out,
    gain_k_out,
    q_in,
    k_in,
    v_in,
    g_in,
    qg_ref,
    kg_ref,
    feat_q,
    feat_k,
    inv_q,
    inv_k,
    rden,
    scaled_hi,
    scaled_lo,
    grad_f,
    gain_row,
    gain_col,
    kt_col,
    part,
    recv_y,
    half,
    recv_w,
    recv_s,
    held,
    full,
    one_a,
    one_b,
    two_a,
    two_b,
    three,
    sizes,
    load_sem,
    send_sem,
    big_recv,
    small_recv,
    far_sem,
):
    tokens = q_in.shape[1]
    dp = lax.axis_index("dp")
    space = lax.axis_index("space")
    y, z = space // Z, space % Z
    k4, g4 = z % 4, z // 4
    sign = 1 - 2 * (dp % 2)

    def at(dy, dz):
        return (dp, lax.rem(y + dy, Y) * Z + lax.rem(z + dz + 2 * Z, Z))

    loads = [
        pltpu.make_async_copy(src, dst, load_sem.at[i])
        for i, (src, dst) in enumerate(
            (
                (k_hbm.at[0], k_in),
                (kg_hbm, kg_ref),
                (qg_hbm, qg_ref),
                (v_hbm.at[0], v_in),
                (q_hbm.at[0], q_in),
                (g_hbm.at[0], g_in),
            )
        )
    ]
    for load in loads:
        load.start()

    barrier = pltpu.get_barrier_semaphore()

    def cluster_peer(r):
        return (dp, lax.rem(y + r // 4, Y) * Z + g4 * 4 + lax.rem(k4 + r % 4, 4))

    greeted = 0
    for r in range(1, 8):
        pl.semaphore_signal(barrier, inc=1, device_id=cluster_peer(r), device_id_type=MESH)
        greeted += 1
    for dy, dz in ((0, 1), (0, -1), (0, 2), (0, -2), (0, 3), (0, -3), (0, 4), (0, -4)):
        pl.semaphore_signal(barrier, inc=1, device_id=at(dy, dz), device_id_type=MESH)
        greeted += 1
    for r in range(1, dps):
        pl.semaphore_signal(
            barrier, inc=1, device_id=(lax.rem(dp + r, dps), space), device_id_type=MESH
        )
        greeted += 1

    lane = lax.broadcasted_iota(jnp.int32, (HEAD_DIM, LANES), 1)
    ones = jnp.ones((16, tokens), BF16)
    no_rows = jnp.zeros((SPARE, tokens), BF16)

    def q_gain(h):
        return gain_col[0:HEAD_DIM, h : h + 1]

    def k_gain(h):
        return gain_col[0:HEAD_DIM, 16 + h : 17 + h]

    def pad(x):
        return jnp.concatenate([x, no_rows], axis=0)

    def features(x_in, inv_ref, gain, feat_ref, h):
        x = x_in[rows_of(h), :].astype(F32)
        inverse = lax.rsqrt(jnp.sum(x * x, axis=0, keepdims=True) * (1.0 / HEAD_DIM) + norm_eps)
        inv_ref[h : h + 1, :] = inverse
        feat = jnp.maximum((x * inverse) * gain(h), 0.0).astype(BF16)
        feat_ref[rows_of(h), :] = feat
        return feat

    def place(a, h, block, spread):
        if h < HOSTS:
            moved = pltpu.roll(spread, (HEAD_DIM - SPARE * h) % LANES, 1)
            block = jnp.where(lane >= HEAD_DIM, moved, block)
        part[a, block_of(h), :] = block

    def take(a, h):
        if h != SPLIT_HEAD:
            return full[a, block_of(h), :][:, 0:HEAD_DIM]
        whole = jnp.zeros((HEAD_DIM, LANES), F32)
        for j in range(HOSTS):
            moved = pltpu.roll(full[a, block_of(j), :], (SPARE * j - HEAD_DIM) % LANES, 1)
            whole = jnp.where((lane >= SPARE * j) & (lane < SPARE * (j + 1)), moved, whole)
        return whole[:, 0:HEAD_DIM]

    order = [SPLIT_HEAD] + [h for h in range(HEADS) if h != SPLIT_HEAD]
    tail = pl.ds((HEADS - 1) * HEAD_DIM, ROWS - (HEADS - 1) * HEAD_DIM)

    sent = [0]

    def go(recv_sem, copies):
        rows = 0
        for src, dst, peer in copies:
            pltpu.make_async_remote_copy(
                src_ref=src,
                dst_ref=dst,
                send_sem=send_sem,
                recv_sem=recv_sem,
                device_id=peer,
                device_id_type=MESH,
            ).start()
            rows += src.shape[0]
        sent[0] += rows
        return recv_sem, rows

    def wait_rows(sem, rows):
        ref = sizes.at[pl.ds(0, rows)]
        pltpu.make_async_copy(ref, ref, sem).wait()

    def land(came):
        wait_rows(*came)

    stride = (4, 12, 8)

    def near(start, size):
        return pl.ds(pl.multiple_of(start, size), size)

    def owner_rows(spot):
        return lax.rem(z + SPOTS[spot] * sign + Z, Z) * OWN

    def spots(first, last):
        return pl.ds(first * OWN, (last - first) * OWN)

    def rs_y(a, p, came):
        src = part.at[a, near(p * PIECE + lax.rem(y + 1, Y) * HALF, HALF)]
        return go(big_recv.at[a, p, 0], [(src, recv_y.at[a, p], at(1, 0))])

    def rs_w(a, p, came):
        land(came)
        base = p * PIECE + y * HALF
        for spot in range(16):
            rows = owner_rows(spot)
            half[a, p, pl.ds(spot * OWN, OWN), :] = (
                part[a, near(base + rows, OWN), :] + recv_y[a, p, near(rows, OWN), :]
            )
        copies, filled = [], 0
        for dz, first, last, _ in HANDS:
            dst = recv_w.at[a, p, spots(filled, filled + last - first)]
            copies.append((half.at[a, p, spots(first, last)], dst, at(0, dz * sign)))
            filled += last - first
        return go(big_recv.at[a, p, 1], copies)

    def rs_s(a, p, came):
        land(came)
        filled = 0
        for dz, first, last, to in HANDS:
            count = last - first
            mine = spots(to, to + count)
            half[a, p, mine, :] = half[a, p, mine, :] + recv_w[a, p, spots(filled, filled + count), :]
            filled += count
        return go(
            big_recv.at[a, p, 2],
            [
                (half.at[a, p, spots(i, i + 1)], recv_s.at[a, p, i], at(0, SPOTS[i] * sign))
                for i in range(COLLECT)
            ],
        )

    def ag_s(a, p, came):
        land(came)
        own = spots(15, 16)
        total = half[a, p, own, :]
        for i in range(COLLECT):
            total = total + recv_s[a, p, i]
        held[a, p, 0, own, :] = total
        return go(
            big_recv.at[a, p, 3],
            [
                (held.at[a, p, 0, own], held.at[a, p, 0, spots(OPPOSITE[i], OPPOSITE[i] + 1)], at(0, SPOTS[i] * sign))
                for i in range(COLLECT)
            ],
        )

    def ag_w(a, p, came):
        land(came)
        copies = []
        for dz, first, last, to in HANDS:
            src = held.at[a, p, 0, spots(to, to + last - first)]
            copies.append((src, held.at[a, p, 0, spots(first, last)], at(0, -dz * sign)))
        return go(big_recv.at[a, p, 4], copies)

    def ag_y(a, p, came):
        land(came)
        came = go(big_recv.at[a, p, 5], [(held.at[a, p, 0], held.at[a, p, 1], at(1, 0))])
        spread_out(a, p, 0, y)
        return came

    def spread_out(a, p, which, side):
        for spot in range(16):
            rows = near(p * PIECE + side * HALF + owner_rows(spot), OWN)
            full[a, rows, :] = held[a, p, which, pl.ds(spot * OWN, OWN), :]

    todo = (rs_y, rs_w, rs_s, ag_s, ag_w, ag_y)
    under_way = {}

    def step(a, *pieces):
        for p in pieces:
            at_stage, came = under_way.get((a, p), (0, None))
            if at_stage < len(todo):
                came = todo[at_stage](a, p, came)
            else:
                land(came)
                spread_out(a, p, 1, lax.rem(y + 1, Y))
            under_way[a, p] = (at_stage + 1, came)

    def small_cluster(slot, buf):
        ref = buf.at[y * 4 + k4]
        return go(small_recv.at[slot], [(ref, ref, cluster_peer(r)) for r in range(1, 8)])

    def small_stride(slot, came, buf_a, buf_b):
        land(came)
        total = buf_a[0]
        for e in range(1, 8):
            total = total + buf_a[e]
        buf_b[g4] = total
        ref = buf_b.at[g4]
        return go(small_recv.at[slot], [(ref, ref, at(0, dz)) for dz in stride])

    def small_done(came, buf_b):
        land(came)
        return (buf_b[0] + buf_b[1]) + (buf_b[2] + buf_b[3])

    cell = y * 4 + k4
    one_a[cell] = jnp.zeros_like(one_a[cell])
    two_a[cell] = jnp.zeros_like(two_a[cell])
    part[0, tail, :] = jnp.zeros((tail.size, LANES), F32)
    part[1, tail, :] = jnp.zeros((tail.size, LANES), F32)

    def after(p):
        done = []
        for h in order[1:]:
            last = block_of(h).start + HEAD_DIM - 1
            if min(last // PIECE, PIECES - 1) == p:
                done.append(h)
        return done

    pieces = range(PIECES)
    A = list(pieces)
    B = []

    def state_blocks(p, spread):
        for h in ([SPLIT_HEAD] if p == 0 else []) + ready[p]:
            block = dot(feat_k[rows_of(h), :], pad(v_in[rows_of(h), :]), NT)
            if h == SPLIT_HEAD:
                spread = block
            else:
                place(0, h, block, spread)
        return spread

    ready = []
    for p in pieces:
        ready.append(
            [
                h
                for h in order[1:]
                if (p - 1 if p else -1) * PIECE + PIECE <= block_of(h).start < (p + 1) * PIECE
            ]
        )

    for load in loads[:3]:
        load.wait()
    gain_row[...] = jnp.ones_like(gain_row)
    for h in range(HEADS):
        cut = pl.ds(h * HEAD_DIM, HEAD_DIM)
        gain_row[h, 0:HEAD_DIM] = qg_ref[cut]
        gain_row[16 + h, 0:HEAD_DIM] = kg_ref[cut]
    gain_col[...] = jnp.transpose(gain_row[...])
    for h in range(HEADS):
        feat = features(k_in, inv_k, k_gain, feat_k, h)
        one_a[cell, h : h + 1, 0:HEAD_DIM] = dot(ones, feat, NT)[0:1]
    pl.semaphore_wait(barrier, greeted)
    for dz in (4, -4):
        pl.semaphore_signal(far_sem, inc=1, device_id=at(0, dz), device_id_type=MESH)
    ar1 = small_cluster(0, one_a)
    loads[3].wait()
    spread = None
    for p in pieces:
        spread = state_blocks(p, spread)
        step(0, p)
    loads[4].wait()
    for h in range(HEADS):
        features(q_in, inv_q, q_gain, feat_q, h)
    step(0, 0)
    pl.semaphore_wait(far_sem, 2)
    ar1 = small_stride(1, ar1, one_a, one_b)
    step(0, *A[1:], *A)

    loads[5].wait()
    key_total = small_done(ar1, one_b)
    kt_col[...] = jnp.transpose(key_total)
    kt_hi, kt_mid = split(key_total)
    kt_lo = (key_total - kt_hi.astype(F32) - kt_mid.astype(F32)).astype(BF16)
    kt3 = jnp.concatenate([kt_hi, kt_mid, kt_lo], axis=0)[:, 0:HEAD_DIM]
    loss_scale = math.sqrt(clip_tokens)

    def grad_state_blocks(p, spread):
        for h in ([SPLIT_HEAD] if p == 0 else []) + ready[p]:
            feat = feat_q[rows_of(h), :]
            terms = dot(kt3, feat, NN)
            denominator = (
                terms[h : h + 1] + (terms[16 + h : 17 + h] + terms[32 + h : 33 + h])
            ) + denom_eps
            inverse = 1.0 / denominator
            rden[h : h + 1, :] = inverse
            scaled = g_in[rows_of(h), :].astype(F32) * (loss_scale * inverse)
            high, low = split(scaled)
            scaled_hi[rows_of(h), :] = high
            scaled_lo[rows_of(h), :] = low
            block = dot(feat, pad(high), NT) + dot(feat, pad(low), NT)
            if h == SPLIT_HEAD:
                spread = block
            else:
                place(1, h, block, spread)
        return spread

    for p in pieces:
        spread = grad_state_blocks(p, spread)
        step(1, p)

    def query_head(h):
        feat = feat_q[rows_of(h), :]
        high, low = scaled_hi[rows_of(h), :], scaled_lo[rows_of(h), :]
        state_hi, state_lo = split(take(0, h))
        grad = dot(state_hi, high, NN) + (dot(state_lo, high, NN) + dot(state_hi, low, NN))
        feat_f = feat.astype(F32)
        projected = jnp.sum(feat_f * grad, axis=0, keepdims=True) * rden[h : h + 1, :]
        grad = grad - kt_col[0:HEAD_DIM, h : h + 1] * projected
        grad_f[rows_of(h), :] = grad
        p_hi, p_lo = split(-projected)
        two_a[cell, HEADS + h : HEADS + h + 1, 0:HEAD_DIM] = (
            dot(jnp.broadcast_to(p_hi, (16, tokens)), feat, NT)
            + dot(jnp.broadcast_to(p_lo, (16, tokens)), feat, NT)
        )[0:1]
        e_hi, e_lo = split(feat_f * grad)
        two_a[cell, h : h + 1, 0:HEAD_DIM] = (
            dot(ones, e_hi, NT) + dot(ones, e_lo, NT)
        )[0:1]

    arrives = [[h for h in after(p)] for p in pieces]
    arrives[-1].append(SPLIT_HEAD)

    last = len(todo)
    order_of_steps = sorted(
        (STAGE_AT[k] + PIECE_GAP * p + GRAD_LAG * a, a, p, k)
        for a, first in ((0, 3), (1, 1))
        for p in pieces
        for k in range(first, last + 1)
    )
    end = order_of_steps.index((STAGE_AT[last] + PIECE_GAP * (PIECES - 1), 0, PIECES - 1, last))
    for _, a, p, k in order_of_steps[: end + 1]:
        step(a, p)
        if a == 0 and k == last:
            for h in arrives[p]:
                query_head(h)
    ar2 = small_cluster(2, two_a)

    def norm_backward(x_in, inv_ref, gain, feat, grad, out, h):
        inverse = inv_ref[h : h + 1, :]
        unit = x_in[rows_of(h), :].astype(F32) * inverse
        upstream = jnp.where(feat > 0, grad, 0.0) * gain(h)
        mean = jnp.sum(upstream * unit, axis=0, keepdims=True) * (1.0 / HEAD_DIM)
        out[0, rows_of(h), :] = (inverse * (upstream - unit * mean)).astype(BF16)

    def grad_queries(heads):
        for h in heads:
            feat = feat_q[rows_of(h), :].astype(F32)
            norm_backward(q_in, inv_q, q_gain, feat, grad_f[rows_of(h), :], out_q, h)

    rest = [(p, k) for _, a, p, k in order_of_steps[end + 1 :]]

    def go_on(stage):
        for p, k in rest:
            if k == stage:
                step(1, p)

    go_on(3)
    grad_queries(range(0, 5))
    go_on(4)
    ar2 = small_stride(3, ar2, two_a, two_b)
    grad_queries(range(5, HEADS))
    go_on(5)

    total = small_done(ar2, two_b)
    three[dp] = total[0:16]
    ref = three.at[dp, pl.ds(0, HEADS)]
    ar3 = go(
        small_recv.at[4], [(ref, ref, (lax.rem(dp + r, dps), space)) for r in range(1, dps)]
    )

    for p in pieces:
        step(1, p)
        for h in arrives[p]:
            gs_hi, gs_lo = split(take(1, h))
            value = v_in[rows_of(h), :]
            feat = feat_k[rows_of(h), :]
            out_v[0, rows_of(h), :] = (dot(gs_hi, feat, TN) + dot(gs_lo, feat, TN)).astype(BF16)
            grad_f[rows_of(h), :] = dot(gs_hi, value, NN) + dot(gs_lo, value, NN)

    gkt_col = jnp.transpose(total)
    for h in range(HEADS):
        feat = feat_k[rows_of(h), :].astype(F32)
        grad = grad_f[rows_of(h), :] + gkt_col[0:HEAD_DIM, HEADS + h : HEADS + h + 1]
        norm_backward(k_in, inv_k, k_gain, feat, grad, out_k, h)

    land(ar3)
    total = three[0]
    for r in range(1, dps):
        total = total + three[r]
    gain_sum = total[0:HEADS, 0:HEAD_DIM] * (1.0 / math.sqrt(all_rows))
    grad_q_gain = gain_sum / gain_row[0:HEADS, 0:HEAD_DIM]
    grad_k_gain = gain_sum / gain_row[16 : 16 + HEADS, 0:HEAD_DIM]
    for h in range(HEADS):
        cut = pl.ds(h * HEAD_DIM, HEAD_DIM)
        gain_q_out[cut] = grad_q_gain[h]
        gain_k_out[cut] = grad_k_gain[h]
    wait_rows(send_sem, sent[0])


def hand_over(*refs):
    sources, results, sem = refs[:5], refs[5:10], refs[10]
    stores = [
        pltpu.make_async_copy(src, dst, sem.at[i])
        for i, (src, dst) in enumerate(zip(sources, results))
    ]
    for store in stores:
        store.start()
    for store in stores:
        store.wait()


def local(queries, keys, values, out_grad, q_gain, k_gain):
    tokens = queries.shape[2]
    dps = lax.axis_size("dp")
    clip_tokens = tokens * lax.axis_size("space")
    all_rows = clip_tokens * dps * queries.shape[0]
    anywhere = pl.BlockSpec(memory_space=pl.ANY)
    big = jax.ShapeDtypeStruct(queries.shape, BF16)
    big_here = pltpu.VMEM(queries.shape, BF16)
    row_here = pltpu.VMEM((CH,), F32)
    here = pl.BlockSpec(memory_space=pltpu.VMEM)
    row = jax.ShapeDtypeStruct((CH,), F32)
    vm = pltpu.VMEM
    dma = pltpu.SemaphoreType.DMA

    def run(*refs):
        kernel(clip_tokens, all_rows, dps, *refs)

    results = pl.pallas_call(
        run,
        out_shape=(big_here, big_here, big_here, row_here, row_here),
        in_specs=[anywhere] * 6,
        out_specs=(here,) * 5,
        scratch_shapes=[
            vm((CH, tokens), BF16),
            vm((CH, tokens), BF16),
            vm((CH, tokens), BF16),
            vm((CH, tokens), BF16),
            vm((CH,), F32),
            vm((CH,), F32),
            vm((CH, tokens), BF16),
            vm((CH, tokens), BF16),
            vm((16, tokens), F32),
            vm((16, tokens), F32),
            vm((16, tokens), F32),
            vm((CH, tokens), BF16),
            vm((CH, tokens), BF16),
            vm((CH, tokens), F32),
            vm((32, LANES), F32),
            vm((LANES, 32), F32),
            vm((LANES, 16), F32),
            vm((2, ROWS, LANES), F32),
            vm((2, PIECES, HALF, LANES), F32),
            vm((2, PIECES, HALF, LANES), F32),
            vm((2, PIECES, 9 * OWN, LANES), F32),
            vm((2, PIECES, COLLECT, OWN, LANES), F32),
            vm((2, PIECES, 2, HALF, LANES), F32),
            vm((2, ROWS, LANES), F32),
            vm((8, 16, LANES), F32),
            vm((4, 16, LANES), F32),
            vm((8, 24, LANES), F32),
            vm((4, 24, LANES), F32),
            vm((dps, 16, LANES), F32),
            vm((2 * 2048 + 640, LANES), F32),
            dma((6,)),
            dma(()),
            dma((2, PIECES, STAGES)),
            dma((5,)),
            pltpu.SemaphoreType.REGULAR,
        ],
        compiler_params=pltpu.CompilerParams(
            collective_id=0, has_side_effects=True, vmem_limit_bytes=VMEM_BYTES
        ),
        name="linear_attention_backward",
    )(queries, keys, values, out_grad, q_gain, k_gain)
    return pl.pallas_call(
        hand_over,
        out_shape=(big, big, big, row, row),
        in_specs=[here] * 5,
        out_specs=(anywhere,) * 5,
        scratch_shapes=[dma((5,))],
        compiler_params=pltpu.CompilerParams(vmem_limit_bytes=4 << 20),
        name="hand_over",
    )(*results)


def solution(mesh):
    whole = P("dp", None, "space")
    return jax.shard_map(
        local,
        mesh=mesh,
        in_specs=(whole, whole, whole, whole, P(), P()),
        out_specs=(whole, whole, whole, P(), P()),
        check_vma=False,
    )
```

```python
import math

import jax
import jax.numpy as jnp
from jax import lax
from jax.experimental import pallas as pl
from jax.experimental.pallas import tpu as pltpu
from jax.sharding import PartitionSpec as P

HEADS = 10
HEAD_DIM = 112
CH = HEADS * HEAD_DIM
LANES = 128
SPLIT_HEAD = 7
SPARE = LANES - HEAD_DIM
HOSTS = HEAD_DIM // SPARE
ROWS = 1024
PIECES = 8
PIECE = ROWS // PIECES
HALF = PIECE // 2
OWN = HALF // 16
STAGES = 6
SPOTS = (-1, -3, -6, 1, 3, 6, -2, -4, -7, -5, -8, 2, 4, 7, 5, 0)
COLLECT = 6
STAGE_AT = (0.0, 3.0, 6.2, 11.7, 17.0, 20.0, 23.2)
PIECE_GAP = 0.45
GRAD_LAG = 10.4
OPPOSITE = (3, 4, 5, 0, 1, 2)
HANDS = ((-1, 6, 9, 0), (-2, 9, 11, 1), (1, 11, 14, 3), (2, 14, 15, 4))
VMEM_BYTES = 62 << 20
Y, Z = 2, 16

norm_eps = 1e-06
denom_eps = 1e-06
F32 = jnp.float32
BF16 = jnp.bfloat16
MESH = pl.DeviceIdType.MESH
NT = (((1,), (1,)), ((), ()))
NN = (((1,), (0,)), ((), ()))
TN = (((0,), (0,)), ((), ()))


def dot(a, b, dims):
    return lax.dot_general(a, b, dims, preferred_element_type=F32)


def split(x):
    high = x.astype(BF16)
    return high, (x - high.astype(F32)).astype(BF16)


def rows_of(head):
    return pl.ds(head * HEAD_DIM, HEAD_DIM)


def block_of(head):
    return pl.ds((head if head < SPLIT_HEAD else head - 1) * HEAD_DIM, HEAD_DIM)


def kernel(
    clip_tokens,
    all_rows,
    dps,
    q_hbm,
    k_hbm,
    v_hbm,
    g_hbm,
    qg_hbm,
    kg_hbm,
    out_q,
    out_k,
    out_v,
    gain_q_out,
    gain_k_out,
    q_in,
    k_in,
    v_in,
    g_in,
    qg_ref,
    kg_ref,
    feat_q,
    feat_k,
    inv_q,
    inv_k,
    rden,
    scaled_hi,
    scaled_lo,
    grad_f,
    gain_row,
    gain_col,
    kt_col,
    part,
    recv_y,
    half,
    recv_w,
    recv_s,
    held,
    full,
    one_a,
    one_b,
    two_a,
    two_b,
    three,
    sizes,
    load_sem,
    send_sem,
    big_recv,
    small_recv,
    far_sem,
):
    tokens = q_in.shape[1]
    dp = lax.axis_index("dp")
    space = lax.axis_index("space")
    y, z = space // Z, space % Z
    k4, g4 = z % 4, z // 4
    sign = 1 - 2 * (dp % 2)

    def at(dy, dz):
        return (dp, lax.rem(y + dy, Y) * Z + lax.rem(z + dz + 2 * Z, Z))

    loads = [
        pltpu.make_async_copy(src, dst, load_sem.at[i])
        for i, (src, dst) in enumerate(
            (
                (k_hbm.at[0], k_in),
                (kg_hbm, kg_ref),
                (qg_hbm, qg_ref),
                (v_hbm.at[0], v_in),
                (q_hbm.at[0], q_in),
                (g_hbm.at[0], g_in),
            )
        )
    ]
    for load in loads:
        load.start()

    barrier = pltpu.get_barrier_semaphore()

    def cluster_peer(r):
        return (dp, lax.rem(y + r // 4, Y) * Z + g4 * 4 + lax.rem(k4 + r % 4, 4))

    greeted = 0
    for r in range(1, 8):
        pl.semaphore_signal(barrier, inc=1, device_id=cluster_peer(r), device_id_type=MESH)
        greeted += 1
    for dy, dz in ((0, 1), (0, -1), (0, 2), (0, -2), (0, 3), (0, -3), (0, 4), (0, -4)):
        pl.semaphore_signal(barrier, inc=1, device_id=at(dy, dz), device_id_type=MESH)
        greeted += 1
    for r in range(1, dps):
        pl.semaphore_signal(
            barrier, inc=1, device_id=(lax.rem(dp + r, dps), space), device_id_type=MESH
        )
        greeted += 1

    lane = lax.broadcasted_iota(jnp.int32, (HEAD_DIM, LANES), 1)
    ones = jnp.ones((16, tokens), BF16)
    no_rows = jnp.zeros((SPARE, tokens), BF16)

    def q_gain(h):
        return gain_col[0:HEAD_DIM, h : h + 1]

    def k_gain(h):
        return gain_col[0:HEAD_DIM, 16 + h : 17 + h]

    def pad(x):
        return jnp.concatenate([x, no_rows], axis=0)

    def features(x_in, inv_ref, gain, feat_ref, h):
        x = x_in[rows_of(h), :].astype(F32)
        inverse = lax.rsqrt(jnp.sum(x * x, axis=0, keepdims=True) * (1.0 / HEAD_DIM) + norm_eps)
        inv_ref[h : h + 1, :] = inverse
        feat = jnp.maximum((x * inverse) * gain(h), 0.0).astype(BF16)
        feat_ref[rows_of(h), :] = feat
        return feat

    def place(a, h, block, spread):
        if h < HOSTS:
            moved = pltpu.roll(spread, (HEAD_DIM - SPARE * h) % LANES, 1)
            block = jnp.where(lane >= HEAD_DIM, moved, block)
        part[a, block_of(h), :] = block

    def take(a, h):
        if h != SPLIT_HEAD:
            return full[a, block_of(h), :][:, 0:HEAD_DIM]
        whole = jnp.zeros((HEAD_DIM, LANES), F32)
        for j in range(HOSTS):
            moved = pltpu.roll(full[a, block_of(j), :], (SPARE * j - HEAD_DIM) % LANES, 1)
            whole = jnp.where((lane >= SPARE * j) & (lane < SPARE * (j + 1)), moved, whole)
        return whole[:, 0:HEAD_DIM]

    order = [SPLIT_HEAD] + [h for h in range(HEADS) if h != SPLIT_HEAD]
    tail = pl.ds((HEADS - 1) * HEAD_DIM, ROWS - (HEADS - 1) * HEAD_DIM)

    sent = [0]

    def go(recv_sem, copies):
        rows = 0
        for src, dst, peer in copies:
            pltpu.make_async_remote_copy(
                src_ref=src,
                dst_ref=dst,
                send_sem=send_sem,
                recv_sem=recv_sem,
                device_id=peer,
                device_id_type=MESH,
            ).start()
            rows += src.shape[0]
        sent[0] += rows
        return recv_sem, rows

    def wait_rows(sem, rows):
        ref = sizes.at[pl.ds(0, rows)]
        pltpu.make_async_copy(ref, ref, sem).wait()

    def land(came):
        wait_rows(*came)

    stride = (4, 12, 8)

    def near(start, size):
        return pl.ds(pl.multiple_of(start, size), size)

    def owner_rows(spot):
        return lax.rem(z + SPOTS[spot] * sign + Z, Z) * OWN

    def spots(first, last):
        return pl.ds(first * OWN, (last - first) * OWN)

    def rs_y(a, p, came):
        src = part.at[a, near(p * PIECE + lax.rem(y + 1, Y) * HALF, HALF)]
        return go(big_recv.at[a, p, 0], [(src, recv_y.at[a, p], at(1, 0))])

    def rs_w(a, p, came):
        land(came)
        base = p * PIECE + y * HALF
        for spot in range(16):
            rows = owner_rows(spot)
            half[a, p, pl.ds(spot * OWN, OWN), :] = (
                part[a, near(base + rows, OWN), :] + recv_y[a, p, near(rows, OWN), :]
            )
        copies, filled = [], 0
        for dz, first, last, _ in HANDS:
            dst = recv_w.at[a, p, spots(filled, filled + last - first)]
            copies.append((half.at[a, p, spots(first, last)], dst, at(0, dz * sign)))
            filled += last - first
        return go(big_recv.at[a, p, 1], copies)

    def rs_s(a, p, came):
        land(came)
        filled = 0
        for dz, first, last, to in HANDS:
            count = last - first
            mine = spots(to, to + count)
            half[a, p, mine, :] = half[a, p, mine, :] + recv_w[a, p, spots(filled, filled + count), :]
            filled += count
        return go(
            big_recv.at[a, p, 2],
            [
                (half.at[a, p, spots(i, i + 1)], recv_s.at[a, p, i], at(0, SPOTS[i] * sign))
                for i in range(COLLECT)
            ],
        )

    def ag_s(a, p, came):
        land(came)
        own = spots(15, 16)
        total = half[a, p, own, :]
        for i in range(COLLECT):
            total = total + recv_s[a, p, i]
        held[a, p, 0, own, :] = total
        return go(
            big_recv.at[a, p, 3],
            [
                (held.at[a, p, 0, own], held.at[a, p, 0, spots(OPPOSITE[i], OPPOSITE[i] + 1)], at(0, SPOTS[i] * sign))
                for i in range(COLLECT)
            ],
        )

    def ag_w(a, p, came):
        land(came)
        copies = []
        for dz, first, last, to in HANDS:
            src = held.at[a, p, 0, spots(to, to + last - first)]
            copies.append((src, held.at[a, p, 0, spots(first, last)], at(0, -dz * sign)))
        return go(big_recv.at[a, p, 4], copies)

    def ag_y(a, p, came):
        land(came)
        came = go(big_recv.at[a, p, 5], [(held.at[a, p, 0], held.at[a, p, 1], at(1, 0))])
        spread_out(a, p, 0, y)
        return came

    def spread_out(a, p, which, side):
        for spot in range(16):
            rows = near(p * PIECE + side * HALF + owner_rows(spot), OWN)
            full[a, rows, :] = held[a, p, which, pl.ds(spot * OWN, OWN), :]

    todo = (rs_y, rs_w, rs_s, ag_s, ag_w, ag_y)
    under_way = {}

    def step(a, *pieces):
        for p in pieces:
            at_stage, came = under_way.get((a, p), (0, None))
            if at_stage < len(todo):
                came = todo[at_stage](a, p, came)
            else:
                land(came)
                spread_out(a, p, 1, lax.rem(y + 1, Y))
            under_way[a, p] = (at_stage + 1, came)

    def small_cluster(slot, buf):
        ref = buf.at[y * 4 + k4]
        return go(small_recv.at[slot], [(ref, ref, cluster_peer(r)) for r in range(1, 8)])

    def small_stride(slot, came, buf_a, buf_b):
        land(came)
        total = buf_a[0]
        for e in range(1, 8):
            total = total + buf_a[e]
        buf_b[g4] = total
        ref = buf_b.at[g4]
        return go(small_recv.at[slot], [(ref, ref, at(0, dz)) for dz in stride])

    def small_done(came, buf_b):
        land(came)
        return (buf_b[0] + buf_b[1]) + (buf_b[2] + buf_b[3])

    cell = y * 4 + k4
    one_a[cell] = jnp.zeros_like(one_a[cell])
    two_a[cell] = jnp.zeros_like(two_a[cell])
    part[0, tail, :] = jnp.zeros((tail.size, LANES), F32)
    part[1, tail, :] = jnp.zeros((tail.size, LANES), F32)

    def after(p):
        done = []
        for h in order[1:]:
            last = block_of(h).start + HEAD_DIM - 1
            if min(last // PIECE, PIECES - 1) == p:
                done.append(h)
        return done

    pieces = range(PIECES)
    A = list(pieces)
    B = []

    def state_blocks(p, spread):
        for h in ([SPLIT_HEAD] if p == 0 else []) + ready[p]:
            block = dot(feat_k[rows_of(h), :], pad(v_in[rows_of(h), :]), NT)
            if h == SPLIT_HEAD:
                spread = block
            else:
                place(0, h, block, spread)
        return spread

    ready = []
    for p in pieces:
        ready.append(
            [
                h
                for h in order[1:]
                if (p - 1 if p else -1) * PIECE + PIECE <= block_of(h).start < (p + 1) * PIECE
            ]
        )

    for load in loads[:3]:
        load.wait()
    gain_row[...] = jnp.ones_like(gain_row)
    for h in range(HEADS):
        cut = pl.ds(h * HEAD_DIM, HEAD_DIM)
        gain_row[h, 0:HEAD_DIM] = qg_ref[cut]
        gain_row[16 + h, 0:HEAD_DIM] = kg_ref[cut]
    gain_col[...] = jnp.transpose(gain_row[...])
    for h in range(HEADS):
        feat = features(k_in, inv_k, k_gain, feat_k, h)
        one_a[cell, h : h + 1, 0:HEAD_DIM] = dot(ones, feat, NT)[0:1]
    pl.semaphore_wait(barrier, greeted)
    for dz in (4, -4):
        pl.semaphore_signal(far_sem, inc=1, device_id=at(0, dz), device_id_type=MESH)
    ar1 = small_cluster(0, one_a)
    loads[3].wait()
    spread = None
    for p in pieces:
        spread = state_blocks(p, spread)
        step(0, p)
    loads[4].wait()
    for h in range(HEADS):
        features(q_in, inv_q, q_gain, feat_q, h)
    step(0, 0)
    pl.semaphore_wait(far_sem, 2)
    ar1 = small_stride(1, ar1, one_a, one_b)
    step(0, *A[1:], *A)

    loads[5].wait()
    key_total = small_done(ar1, one_b)
    kt_col[...] = jnp.transpose(key_total)
    kt_hi, kt_mid = split(key_total)
    kt_lo = (key_total - kt_hi.astype(F32) - kt_mid.astype(F32)).astype(BF16)
    kt3 = jnp.concatenate([kt_hi, kt_mid, kt_lo], axis=0)[:, 0:HEAD_DIM]
    loss_scale = math.sqrt(clip_tokens)

    def grad_state_blocks(p, spread):
        for h in ([SPLIT_HEAD] if p == 0 else []) + ready[p]:
            feat = feat_q[rows_of(h), :]
            terms = dot(kt3, feat, NN)
            denominator = (
                terms[h : h + 1] + (terms[16 + h : 17 + h] + terms[32 + h : 33 + h])
            ) + denom_eps
            inverse = 1.0 / denominator
            rden[h : h + 1, :] = inverse
            scaled = g_in[rows_of(h), :].astype(F32) * (loss_scale * inverse)
            high, low = split(scaled)
            scaled_hi[rows_of(h), :] = high
            scaled_lo[rows_of(h), :] = low
            block = dot(feat, pad(high), NT) + dot(feat, pad(low), NT)
            if h == SPLIT_HEAD:
                spread = block
            else:
                place(1, h, block, spread)
        return spread

    for p in pieces:
        spread = grad_state_blocks(p, spread)
        step(1, p)

    def query_head(h):
        feat = feat_q[rows_of(h), :]
        high, low = scaled_hi[rows_of(h), :], scaled_lo[rows_of(h), :]
        state_hi, state_lo = split(take(0, h))
        grad = dot(state_hi, high, NN) + (dot(state_lo, high, NN) + dot(state_hi, low, NN))
        feat_f = feat.astype(F32)
        projected = jnp.sum(feat_f * grad, axis=0, keepdims=True) * rden[h : h + 1, :]
        grad = grad - kt_col[0:HEAD_DIM, h : h + 1] * projected
        grad_f[rows_of(h), :] = grad
        p_hi, p_lo = split(-projected)
        two_a[cell, HEADS + h : HEADS + h + 1, 0:HEAD_DIM] = (
            dot(jnp.broadcast_to(p_hi, (16, tokens)), feat, NT)
            + dot(jnp.broadcast_to(p_lo, (16, tokens)), feat, NT)
        )[0:1]
        e_hi, e_lo = split(feat_f * grad)
        two_a[cell, h : h + 1, 0:HEAD_DIM] = (
            dot(ones, e_hi, NT) + dot(ones, e_lo, NT)
        )[0:1]

    arrives = [[h for h in after(p)] for p in pieces]
    arrives[-1].append(SPLIT_HEAD)

    last = len(todo)
    order_of_steps = sorted(
        (STAGE_AT[k] + PIECE_GAP * p + GRAD_LAG * a, a, p, k)
        for a, first in ((0, 3), (1, 1))
        for p in pieces
        for k in range(first, last + 1)
    )
    end = order_of_steps.index((STAGE_AT[last] + PIECE_GAP * (PIECES - 1), 0, PIECES - 1, last))
    for _, a, p, k in order_of_steps[: end + 1]:
        step(a, p)
        if a == 0 and k == last:
            for h in arrives[p]:
                query_head(h)
    ar2 = small_cluster(2, two_a)

    def norm_backward(x_in, inv_ref, gain, feat, grad, out, h):
        inverse = inv_ref[h : h + 1, :]
        unit = x_in[rows_of(h), :].astype(F32) * inverse
        upstream = jnp.where(feat > 0, grad, 0.0) * gain(h)
        mean = jnp.sum(upstream * unit, axis=0, keepdims=True) * (1.0 / HEAD_DIM)
        out[0, rows_of(h), :] = (inverse * (upstream - unit * mean)).astype(BF16)

    def grad_queries(heads):
        for h in heads:
            feat = feat_q[rows_of(h), :].astype(F32)
            norm_backward(q_in, inv_q, q_gain, feat, grad_f[rows_of(h), :], out_q, h)

    rest = [(p, k) for _, a, p, k in order_of_steps[end + 1 :]]

    def go_on(stage):
        for p, k in rest:
            if k == stage:
                step(1, p)

    go_on(3)
    grad_queries(range(0, 5))
    go_on(4)
    ar2 = small_stride(3, ar2, two_a, two_b)
    grad_queries(range(5, HEADS))
    go_on(5)

    total = small_done(ar2, two_b)
    three[dp] = total[0:16]
    ref = three.at[dp, pl.ds(0, HEADS)]
    ar3 = go(
        small_recv.at[4], [(ref, ref, (lax.rem(dp + r, dps), space)) for r in range(1, dps)]
    )

    for p in pieces:
        step(1, p)
        for h in arrives[p]:
            gs_hi, gs_lo = split(take(1, h))
            value = v_in[rows_of(h), :]
            feat = feat_k[rows_of(h), :]
            out_v[0, rows_of(h), :] = (dot(gs_hi, feat, TN) + dot(gs_lo, feat, TN)).astype(BF16)
            grad_f[rows_of(h), :] = dot(gs_hi, value, NN) + dot(gs_lo, value, NN)

    gkt_col = jnp.transpose(total)
    for h in range(HEADS):
        feat = feat_k[rows_of(h), :].astype(F32)
        grad = grad_f[rows_of(h), :] + gkt_col[0:HEAD_DIM, HEADS + h : HEADS + h + 1]
        norm_backward(k_in, inv_k, k_gain, feat, grad, out_k, h)

    land(ar3)
    total = three[0]
    for r in range(1, dps):
        total = total + three[r]
    gain_sum = total[0:HEADS, 0:HEAD_DIM] * (1.0 / math.sqrt(all_rows))
    grad_q_gain = gain_sum / gain_row[0:HEADS, 0:HEAD_DIM]
    grad_k_gain = gain_sum / gain_row[16 : 16 + HEADS, 0:HEAD_DIM]
    for h in range(HEADS):
        cut = pl.ds(h * HEAD_DIM, HEAD_DIM)
        gain_q_out[cut] = grad_q_gain[h]
        gain_k_out[cut] = grad_k_gain[h]
    wait_rows(send_sem, sent[0])


def hand_over(*refs):
    sources, results, sem = refs[:5], refs[5:10], refs[10]
    stores = [
        pltpu.make_async_copy(src, dst, sem.at[i])
        for i, (src, dst) in enumerate(zip(sources, results))
    ]
    for store in stores:
        store.start()
    for store in stores:
        store.wait()


def local(queries, keys, values, out_grad, q_gain, k_gain):
    tokens = queries.shape[2]
    dps = lax.axis_size("dp")
    clip_tokens = tokens * lax.axis_size("space")
    all_rows = clip_tokens * dps * queries.shape[0]
    anywhere = pl.BlockSpec(memory_space=pl.ANY)
    big = jax.ShapeDtypeStruct(queries.shape, BF16)
    big_here = pltpu.VMEM(queries.shape, BF16)
    row_here = pltpu.VMEM((CH,), F32)
    here = pl.BlockSpec(memory_space=pltpu.VMEM)
    row = jax.ShapeDtypeStruct((CH,), F32)
    vm = pltpu.VMEM
    dma = pltpu.SemaphoreType.DMA

    def run(*refs):
        kernel(clip_tokens, all_rows, dps, *refs)

    results = pl.pallas_call(
        run,
        out_shape=(big_here, big_here, big_here, row_here, row_here),
        in_specs=[anywhere] * 6,
        out_specs=(here,) * 5,
        scratch_shapes=[
            vm((CH, tokens), BF16),
            vm((CH, tokens), BF16),
            vm((CH, tokens), BF16),
            vm((CH, tokens), BF16),
            vm((CH,), F32),
            vm((CH,), F32),
            vm((CH, tokens), BF16),
            vm((CH, tokens), BF16),
            vm((16, tokens), F32),
            vm((16, tokens), F32),
            vm((16, tokens), F32),
            vm((CH, tokens), BF16),
            vm((CH, tokens), BF16),
            vm((CH, tokens), F32),
            vm((32, LANES), F32),
            vm((LANES, 32), F32),
            vm((LANES, 16), F32),
            vm((2, ROWS, LANES), F32),
            vm((2, PIECES, HALF, LANES), F32),
            vm((2, PIECES, HALF, LANES), F32),
            vm((2, PIECES, 9 * OWN, LANES), F32),
            vm((2, PIECES, COLLECT, OWN, LANES), F32),
            vm((2, PIECES, 2, HALF, LANES), F32),
            vm((2, ROWS, LANES), F32),
            vm((8, 16, LANES), F32),
            vm((4, 16, LANES), F32),
            vm((8, 24, LANES), F32),
            vm((4, 24, LANES), F32),
            vm((dps, 16, LANES), F32),
            vm((2 * 2048 + 640, LANES), F32),
            dma((6,)),
            dma(()),
            dma((2, PIECES, STAGES)),
            dma((5,)),
            pltpu.SemaphoreType.REGULAR,
        ],
        compiler_params=pltpu.CompilerParams(
            collective_id=0, has_side_effects=True, vmem_limit_bytes=VMEM_BYTES
        ),
        name="linear_attention_backward",
    )(queries, keys, values, out_grad, q_gain, k_gain)
    return pl.pallas_call(
        hand_over,
        out_shape=(big, big, big, row, row),
        in_specs=[here] * 5,
        out_specs=(anywhere,) * 5,
        scratch_shapes=[dma((5,))],
        compiler_params=pltpu.CompilerParams(vmem_limit_bytes=4 << 20),
        name="hand_over",
    )(*results)


def solution(mesh):
    whole = P("dp", None, "space")
    return jax.shard_map(
        local,
        mesh=mesh,
        in_specs=(whole, whole, whole, whole, P(), P()),
        out_specs=(whole, whole, whole, P(), P()),
        check_vma=False,
    )
```
